32 devices in a mesh: ctx: 8 (over z, x), tensor: 2 (over core), dp: 2 (over y).
Axes of the slice: x: 2, y: 2, z: 4, core: 2. Of those that a mesh axis runs over, the one named last changes fastest.
Arguments:
- cache: bfloat16 [8, 8, 4096, 256], P('dp', 'tensor', 'ctx'), may hold values from -6 to 6
- kept: int32 [8, 8, 1024], P('dp', 'tensor'), may hold values from 0 to 4095, as said below
- assign: int32 [8], replicated, may hold values from 0 to 7, each once
- queries: bfloat16 [8, 128, 8192], P('ctx', 'dp', 'tensor'), may hold values from -140 to 140
- new_kv: bfloat16 [8, 128, 8, 256], P('ctx', 'dp', 'tensor'), may hold values from -5 to 5
- out_weight: bfloat16 [8192, 8192], P('tensor', 'ctx'), may hold values from -0.0625 to 0.0625
Outputs:
- output: bfloat16 [8, 128, 8192], P('tensor', 'dp', 'ctx')
The draws below stay inside these ranges and needn't reach their ends.
Inputs may be any that keep to these rules, and one draw needn't show every extreme that they name: Each kept[p, t] lists 1024 distinct positions in increasing order; block b holds positions b * 512 to (b + 1) * 512 - 1; at most 256 positions of one list fall in one block, and in every list some block holds exactly 256. `assign`: every slot 0 to 7 is given to exactly one prompt.
All inputs are finite; a program needn't handle non-finite values.
Results may differ from the reference program's by a relative error of at most 0.029.
Values may be sent and summed in bfloat16 or wider, within the bound.
A program may use at most 64 MiB of HBM per device.

```python
import jax
import jax.numpy as jnp
from jax import lax

D = 8192
QH = 64
KVH = 8
HD = 128
CTX_DEV = 512
NEW = 128
PROMPTS = 8
LEN = 4096
KEEP = 1024


def shared_keys(key):
    return jnp.clip(jax.random.normal(key, (PROMPTS, NEW, KVH, HD), jnp.float32), -5.0, 5.0)


def draw_new_kv(key, part):
    base_keys = shared_keys(key)
    key = jax.random.fold_in(key, 11)
    value_key = jax.random.fold_in(key, 0)
    values = jnp.clip(jax.random.normal(value_key, (PROMPTS, NEW, KVH, HD), jnp.float32), -5.0, 5.0)
    return jnp.concatenate([base_keys, values], axis=3).astype(jnp.bfloat16)


def draw_queries(key, part):
    key = jax.random.fold_in(key, 7)
    draw_shape = (PROMPTS, NEW, KVH, QH // KVH, HD)
    values = jnp.clip(2.0 * jax.random.normal(key, draw_shape, jnp.float32), -12.0, 12.0)
    return values.reshape(PROMPTS, NEW, QH * HD).astype(jnp.bfloat16)


def draw_kept(key, part):
    key = jax.random.fold_in(key, 3)
    blocks = LEN // CTX_DEV
    mean_count = CTX_DEV // 4
    pair_key, order_key, spot_key = jax.random.split(key, 3)
    shifts = jax.random.randint(pair_key, (PROMPTS, KVH, blocks // 2), 0, mean_count + 1)
    shifts = shifts.at[:, :, 0].set(mean_count)
    paired = jnp.concatenate([mean_count + shifts, mean_count - shifts], axis=2)
    order_scores = jax.random.randint(order_key, (PROMPTS, KVH, blocks), 0, 1 << 20) * blocks + jnp.arange(blocks)
    block_order = jnp.argsort(order_scores, axis=2)
    counts = jnp.take_along_axis(paired, block_order, axis=2)
    spot_scores = jax.random.randint(spot_key, (PROMPTS, KVH, blocks, CTX_DEV), 0, 1 << 10) * CTX_DEV + jnp.arange(CTX_DEV)
    spot_rank = jnp.argsort(jnp.argsort(spot_scores, axis=3), axis=3)
    chosen = spot_rank < counts[..., None]
    positions = jnp.arange(LEN, dtype=jnp.int32).reshape(blocks, CTX_DEV)
    keyed = jnp.where(chosen, positions, positions + LEN).reshape(PROMPTS, KVH, LEN)
    return jnp.sort(keyed, axis=2)[:, :, :KEEP].astype(jnp.int32)


def steps_of(stream_key, dims, shards, low, top_value):
    level = 1.0
    for dim, shards_of in shards:
        steps = jax.random.uniform(jax.random.fold_in(jax.random.fold_in(stream_key, 6), dim), (shards_of,), jnp.float32, low / len(shards), top_value / len(shards))
        level = level * jnp.repeat(jnp.exp(steps), dims[dim] // shards_of).reshape((-1,) + (1,) * (len(dims) - 1 - dim))
    return level


def gaussian(stream_key, extent, spread, reach, shards=(), kind=jnp.bfloat16):
    drawn = spread * jax.random.normal(stream_key, extent, jnp.float32)
    if shards:
        drawn = drawn * steps_of(stream_key, extent, shards, -0.22, 0.18)
    return jnp.clip(drawn, -reach, reach).astype(kind)


def setup_inputs(seed: int = 0) -> dict:
    keys = jax.random.split(jax.random.key(seed), 7)
    return {
        "cache": gaussian(keys[0], (PROMPTS, KVH, LEN, 2 * HD), 1.0, 6.0, ((0, 2), (1, 2), (2, 8))),
        "kept": draw_kept(jax.random.fold_in(keys[6], 71), 0),
        "assign": jax.random.permutation(keys[2], PROMPTS).astype(jnp.int32),
        "queries": draw_queries(jax.random.fold_in(keys[6], 71), 0),
        "new_kv": draw_new_kv(jax.random.fold_in(keys[6], 71), 0),
        "out_weight": gaussian(keys[5], (QH * HD, D), (QH * HD) ** -0.5, 0.0625, ((0, 2), (1, 8))),
    }


def take_kept(block_rows, picked):
    return block_rows[picked]


def reference(cache, kept, assign, queries, new_kv, out_weight):
    per_group = QH // KVH
    score_scale = HD ** -0.5

    def one_prompt(index):
        slot_id = assign[index]
        prompt_cache = lax.dynamic_index_in_dim(cache, index, 0, keepdims=False)
        kept_lists = lax.dynamic_index_in_dim(kept, index, 0, keepdims=False)
        kept_rows = jax.vmap(take_kept)(prompt_cache, kept_lists)
        query = lax.dynamic_index_in_dim(queries, slot_id, 0, keepdims=False).reshape(NEW, KVH, per_group, HD)
        fresh_rows = jnp.transpose(lax.dynamic_index_in_dim(new_kv, slot_id, 0, keepdims=False), (1, 0, 2))
        kept_cache = jnp.concatenate([kept_rows, fresh_rows], axis=1)
        query_wide = query.astype(jnp.float32)
        keys_wide = kept_cache[:, :, :HD].astype(jnp.float32)
        values_wide = kept_cache[:, :, HD:].astype(jnp.float32)
        scores = jnp.einsum("rkgd,knd->kgrn", query_wide, keys_wide) * score_scale
        key_ids = jnp.arange(KEEP + NEW, dtype=jnp.int32) - KEEP
        row_ids = jnp.arange(NEW, dtype=jnp.int32)
        visible = key_ids[None, :] <= row_ids[:, None]
        row_top = jnp.max(jnp.where(visible, scores, -jnp.inf), axis=3, keepdims=True)
        weights = jnp.exp(jnp.where(visible, scores - row_top, -jnp.inf))
        weight_sum = jnp.sum(weights, axis=3)
        rounded = lax.optimization_barrier(weights.astype(jnp.bfloat16)).astype(jnp.float32)
        weighted = jnp.einsum("kgrn,knd->rkgd", rounded, values_wide)
        head_out = (weighted / jnp.transpose(weight_sum, (2, 0, 1))[..., None]).reshape(NEW, QH * HD).astype(jnp.bfloat16)
        return jnp.dot(head_out, out_weight, preferred_element_type=jnp.float32).astype(jnp.bfloat16)

    return lax.map(one_prompt, jnp.arange(PROMPTS, dtype=jnp.int32))
```

```python
import functools
import math

import jax
import jax.numpy as jnp
from jax import lax
from jax.experimental import pallas as pl
from jax.experimental.pallas import tpu as pltpu
from jax.sharding import PartitionSpec as P

neg_large = -1e30


def swapped(array, axis, distance):
    return lax.ppermute(array, axis, [(i, i ^ 1 << distance) for i in range(lax.axis_size(axis))])


def slot_prompt(assign, slot_id):
    matches = (assign == slot_id).astype(jnp.int32)
    return jnp.sum(matches * jnp.arange(assign.shape[0], dtype=jnp.int32))


def block_rows_of(flat_cache, kept_lists, block_start, first_rank, row_count, stride, capacity):
    offsets = jnp.arange(capacity, dtype=jnp.int32)
    rank_ids = jnp.clip(first_rank[:, None] + stride * offsets[None, :], 0, kept_lists.shape[1] - 1)
    places = jnp.take_along_axis(kept_lists, rank_ids, axis=1) - block_start
    is_valid = offsets[None, :] < row_count[:, None]
    spots = jnp.arange(flat_cache.shape[1], dtype=jnp.int32)
    chooser = ((places[:, :, None] == spots[None, None, :]) & is_valid[:, :, None]).astype(
        flat_cache.dtype
    )
    picked = jnp.einsum("gcq,gqw->gcw", chooser, flat_cache, preferred_element_type=jnp.float32)
    return picked.astype(flat_cache.dtype)


def padded_layout(rows, marks):
    senders, kv_here, capacity, row_width = rows.shape
    flat_rows = jnp.transpose(rows, (1, 0, 2, 3)).reshape(kv_here, senders * capacity, row_width)
    flat_marks = jnp.transpose(marks, (1, 0, 2)).reshape(kv_here, senders * capacity)
    return (flat_rows, flat_marks)


def attend_rows(query, row_start, kept_rows, kept_marks, new_rows, new_start):
    head_dim = kept_rows.shape[2] // 2
    score_scale = head_dim ** (-0.5)
    kept_scores = (
        jnp.einsum(
            "rkgd,knd->rkgn", query, kept_rows[:, :, :head_dim], preferred_element_type=jnp.float32
        )
        * score_scale
    )
    kept_scores = jnp.where((kept_marks > 0.5)[None, :, None, :], kept_scores, neg_large)
    new_scores = (
        jnp.einsum(
            "rkgd,nkd->rkgn", query, new_rows[:, :, :head_dim], preferred_element_type=jnp.float32
        )
        * score_scale
    )
    row_ids = row_start + jnp.arange(query.shape[0], dtype=jnp.int32)
    key_ids = new_start + jnp.arange(new_rows.shape[0], dtype=jnp.int32)
    visible = (key_ids[None, :] <= row_ids[:, None])[:, None, None, :]
    new_scores = jnp.where(visible, new_scores, neg_large)
    row_top = jnp.maximum(jnp.max(kept_scores, axis=3), jnp.max(new_scores, axis=3))
    kept_weights = jnp.exp(kept_scores - row_top[..., None])
    new_weights = jnp.exp(new_scores - row_top[..., None])
    weight_sum = jnp.sum(kept_weights, axis=3) + jnp.sum(new_weights, axis=3)
    weighted = jnp.einsum(
        "rkgn,knd->rkgd",
        kept_weights.astype(jnp.bfloat16),
        kept_rows[:, :, head_dim:],
        preferred_element_type=jnp.float32,
    )
    weighted = weighted + jnp.einsum(
        "rkgn,nkd->rkgd",
        new_weights.astype(jnp.bfloat16),
        new_rows[:, :, head_dim:],
        preferred_element_type=jnp.float32,
    )
    return (row_top, weight_sum, weighted)


def attend(query, row_start, kept_rows, kept_marks, new_rows, new_start):
    half_rows = query.shape[0] // 2
    first = attend_rows(query[:half_rows], row_start, kept_rows, kept_marks, new_rows, new_start)
    second = attend_rows(
        query[half_rows:], row_start + half_rows, kept_rows, kept_marks, new_rows, new_start
    )
    return tuple((jnp.concatenate([first[index], second[index]], axis=0) for index in range(3)))


def local_by_rows(cache, kept, assign, queries, new_kv, out_weight):
    ctx_count = lax.axis_size("ctx")
    ctx_id = lax.axis_index("ctx")
    dp_id = lax.axis_index("dp")
    groups, kv_here, ctx_dev, row_width = cache.shape
    head_dim = row_width // 2
    keep_total = kept.shape[2]
    flat_cache = cache.reshape(groups * kv_here, ctx_dev, row_width)
    kept_lists = kept.reshape(groups * kv_here, keep_total)
    block_start = ctx_id * ctx_dev
    rank_low = jnp.sum((kept_lists < block_start).astype(jnp.int32), axis=1)
    rank_high = jnp.sum((kept_lists < block_start + ctx_dev).astype(jnp.int32), axis=1)
    slot_ids = lax.dynamic_slice_in_dim(assign, dp_id * groups, groups)
    prompt = slot_prompt(assign, ctx_id)
    capacity = ctx_dev // 2
    row_count = rank_high - rank_low
    picked = block_rows_of(flat_cache, kept_lists, block_start, rank_low, row_count, 1, capacity)
    picked = picked.reshape(groups, kv_here, capacity, row_width)
    buffer = (
        jnp.zeros((ctx_count, kv_here, capacity, row_width), cache.dtype).at[slot_ids].set(picked)
    )
    counts = (
        jnp.zeros((ctx_count, kv_here), jnp.int32)
        .at[slot_ids]
        .set(row_count.reshape(groups, kv_here))
    )
    received, got_counts = (
        lax.all_to_all(buffer, "ctx", split_axis=0, concat_axis=0, tiled=True),
        lax.all_to_all(counts, "ctx", split_axis=0, concat_axis=0, tiled=True),
    )
    halves = received.reshape(ctx_count, kv_here, capacity // 2, 2, row_width)
    offsets = jnp.arange(capacity // 2, dtype=jnp.int32)
    even_marks = (2 * offsets[None, None, :] < got_counts[:, :, None]).astype(cache.dtype)
    odd_marks = (2 * offsets[None, None, :] + 1 < got_counts[:, :, None]).astype(cache.dtype)
    own_rows = jnp.where(dp_id == 0, halves[:, :, :, 0], halves[:, :, :, 1])
    own_marks = jnp.where(dp_id == 0, even_marks, odd_marks)
    their_rows = jnp.where(dp_id == 0, halves[:, :, :, 1], halves[:, :, :, 0])
    their_marks = jnp.where(dp_id == 0, odd_marks, even_marks)
    own_flat, own_flat_marks = padded_layout(own_rows, own_marks)
    their_flat, their_flat_marks = padded_layout(their_rows, their_marks)
    from_partner, partner_marks = swapped((their_flat, their_flat_marks), "dp", 0)
    owner_here = prompt // groups == dp_id
    kept_half = jnp.where(owner_here, own_flat, from_partner)
    kept_marks = jnp.where(owner_here, own_flat_marks, partner_marks)
    rows_here = queries.shape[1]
    per_group = queries.shape[2] // (kv_here * head_dim)
    own_query = queries[0].reshape(rows_here, kv_here, per_group, head_dim)
    own_new = new_kv[0]
    own_start = dp_id * rows_here
    other_kept, other_marks, other_new = swapped((kept_half, kept_marks, own_new), "dp", 0)
    all_kept = jnp.concatenate([kept_half, other_kept], axis=1)
    all_marks = jnp.concatenate([kept_marks, other_marks], axis=1)
    all_new = jnp.where(
        dp_id == 0,
        jnp.concatenate([own_new, other_new], axis=0),
        jnp.concatenate([other_new, own_new], axis=0),
    )
    row_top, weight_sum, weighted = attend(own_query, own_start, all_kept, all_marks, all_new, 0)
    head_out = (
        (weighted / weight_sum[..., None])
        .reshape(rows_here, kv_here * per_group * head_dim)
        .astype(jnp.bfloat16)
    )
    partials = jnp.dot(
        lax.all_gather(head_out, "ctx", axis=0, tiled=True),
        out_weight,
        preferred_element_type=jnp.float32,
    )
    partials = partials.reshape(ctx_count, rows_here, partials.shape[1])[assign]
    return lax.psum_scatter(
        partials.astype(jnp.bfloat16), "tensor", scatter_dimension=0, tiled=True
    )


def select_kernel(start_ref, kept_ref, cache_ref, out_ref):
    start = start_ref[0]
    kept = kept_ref[0]
    total = kept.shape[1]
    spots = cache_ref.shape[1]
    capacity = out_ref.shape[1]
    first = jnp.sum((kept < start).astype(jnp.int32))
    wide = jnp.broadcast_to(kept, (8, total))
    places = pltpu.roll(wide, lax.rem(total - first, total), 1)[:1, :capacity] - start
    spot_ids = lax.broadcasted_iota(jnp.int32, (spots, capacity), 0)
    chooser = (spot_ids == places).astype(jnp.float32).astype(jnp.bfloat16)
    picked = lax.dot_general(
        chooser, cache_ref[0], (((0,), (0,)), ((), ())), preferred_element_type=jnp.float32
    )
    out_ref[0] = picked.astype(out_ref.dtype)


def select_rows(flat_cache, kept_lists, block_start, capacity):
    lists, spots, width = flat_cache.shape
    total = kept_lists.shape[1]
    return pl.pallas_call(
        select_kernel,
        out_shape=jax.ShapeDtypeStruct((lists, capacity, width), flat_cache.dtype),
        grid_spec=pltpu.PrefetchScalarGridSpec(
            num_scalar_prefetch=1,
            grid=(lists,),
            in_specs=[
                pl.BlockSpec((1, 1, total), lambda i, s: (i, 0, 0)),
                pl.BlockSpec((1, spots, width), lambda i, s: (i, 0, 0)),
            ],
            out_specs=pl.BlockSpec((1, capacity, width), lambda i, s: (i, 0, 0)),
        ),
    )(block_start.reshape(1), kept_lists.reshape(lists, 1, total), flat_cache)


def arrange_kernel(groups, order_ref, dp_ref, mine_ref, got_ref, out_ref):
    from_mine = order_ref[pl.program_id(0)] // groups == dp_ref[0]

    @pl.when(from_mine)
    def _():
        out_ref[...] = mine_ref[...]

    @pl.when(jnp.logical_not(from_mine))
    def _():
        out_ref[...] = got_ref[...]


def arrange(mine, got, order, dp_id):
    groups, heads, capacity, width = mine.shape
    block = (1, heads, capacity, width)

    def source(i, order_ref, dp_ref):
        return (order_ref[i] % groups, 0, 0, 0)

    return pl.pallas_call(
        functools.partial(arrange_kernel, groups),
        out_shape=jax.ShapeDtypeStruct((order.shape[0], heads, capacity, width), mine.dtype),
        grid_spec=pltpu.PrefetchScalarGridSpec(
            num_scalar_prefetch=2,
            grid=(order.shape[0],),
            in_specs=[pl.BlockSpec(block, source), pl.BlockSpec(block, source)],
            out_specs=pl.BlockSpec(block, lambda i, a, b: (i, 0, 0, 0)),
        ),
    )(order, dp_id.reshape(1), mine, got)


def attend_kernel(q_ref, rows_ref, bias_ref, new_ref, out_ref):
    blocks, _, capacity, width = rows_ref.shape
    hd = width // 2
    rows = q_ref.shape[0]
    q = jnp.concatenate([q_ref[:, :hd], q_ref[:, hd:]], axis=0)
    keys = rows_ref[:, 0, :, :hd].reshape(blocks * capacity, hd)
    values = rows_ref[:, 0, :, hd:].reshape(blocks * capacity, hd)
    new_keys = new_ref[0, :, :hd]
    new_values = new_ref[0, :, hd:]
    scale = hd**-0.5 * math.log2(math.e)
    dims = (((1,), (1,)), ((), ()))
    kept_scores = lax.dot_general(q, keys, dims, preferred_element_type=jnp.float32) * scale
    kept_scores = kept_scores + bias_ref[0]
    new_scores = lax.dot_general(q, new_keys, dims, preferred_element_type=jnp.float32) * scale
    row_ids = lax.rem(lax.broadcasted_iota(jnp.int32, new_scores.shape, 0), rows)
    key_ids = lax.broadcasted_iota(jnp.int32, new_scores.shape, 1)
    new_scores = jnp.where(key_ids <= row_ids, new_scores, neg_large)
    top = jnp.maximum(
        jnp.max(kept_scores, axis=1, keepdims=True), jnp.max(new_scores, axis=1, keepdims=True)
    )
    kept_weights = jnp.exp2(kept_scores - top)
    new_weights = jnp.exp2(new_scores - top)
    total = jnp.sum(kept_weights, axis=1, keepdims=True) + jnp.sum(new_weights, axis=1, keepdims=True)
    weighted = jnp.dot(
        kept_weights.astype(jnp.bfloat16), values, preferred_element_type=jnp.float32
    ) + jnp.dot(new_weights.astype(jnp.bfloat16), new_values, preferred_element_type=jnp.float32)
    result = (weighted / total).astype(out_ref.dtype)
    out_ref[:, :hd] = result[:rows]
    out_ref[:, hd:] = result[rows:]


def attend_heads(query, received, bias, new_rows, per_group):
    rows, columns = query.shape
    blocks, heads, capacity, width = received.shape
    hd = width // 2
    pairs = per_group // 2
    return pl.pallas_call(
        attend_kernel,
        out_shape=jax.ShapeDtypeStruct(query.shape, query.dtype),
        grid=(heads, pairs),
        in_specs=[
            pl.BlockSpec((rows, 2 * hd), lambda h, j: (0, h * pairs + j)),
            pl.BlockSpec((blocks, 1, capacity, width), lambda h, j: (0, h, 0, 0)),
            pl.BlockSpec((1, 1, blocks * capacity), lambda h, j: (h, 0, 0)),
            pl.BlockSpec((1, rows, width), lambda h, j: (h, 0, 0)),
        ],
        out_specs=pl.BlockSpec((rows, 2 * hd), lambda h, j: (0, h * pairs + j)),
        compiler_params=pltpu.CompilerParams(vmem_limit_bytes=48 * 1024 * 1024),
    )(query, received, bias, new_rows)


def project_kernel(assign_ref, heads_ref, weight_ref, out_ref, lhs):
    prompts, rows, _ = heads_ref.shape

    @pl.when(pl.program_id(0) == 0)
    def _():
        for p in range(prompts):
            lhs[p * rows : (p + 1) * rows] = heads_ref[assign_ref[p]]

    product = jnp.dot(lhs[...], weight_ref[...], preferred_element_type=jnp.float32)
    out_ref[...] = product.astype(out_ref.dtype).reshape(out_ref.shape)


def project(gathered, out_weight, assign):
    prompts, rows, depth = gathered.shape
    columns = out_weight.shape[1]
    tile = min(256, columns)
    return pl.pallas_call(
        project_kernel,
        out_shape=jax.ShapeDtypeStruct((prompts, rows, columns), gathered.dtype),
        grid_spec=pltpu.PrefetchScalarGridSpec(
            num_scalar_prefetch=1,
            grid=(columns // tile,),
            in_specs=[
                pl.BlockSpec((prompts, rows, depth), lambda i, a: (0, 0, 0)),
                pl.BlockSpec((depth, tile), lambda i, a: (0, i)),
            ],
            out_specs=pl.BlockSpec((prompts, rows, tile), lambda i, a: (0, 0, i)),
            scratch_shapes=[pltpu.VMEM((prompts * rows, depth), gathered.dtype)],
        ),
        compiler_params=pltpu.CompilerParams(vmem_limit_bytes=48 * 1024 * 1024),
    )(assign, gathered, out_weight)


def in_dp_order(own, other, dp_id, axis):
    return jnp.where(
        dp_id == 0,
        jnp.concatenate([own, other], axis=axis),
        jnp.concatenate([other, own], axis=axis),
    )


def halves_of(array, dp_id, axis):
    size = array.shape[axis] // 2
    mine = lax.dynamic_slice_in_dim(array, dp_id * size, size, axis)
    theirs = lax.dynamic_slice_in_dim(array, (1 - dp_id) * size, size, axis)
    return mine, theirs


def prepare(cache, kept, assign, queries, new_kv):
    ctx_count = lax.axis_size("ctx")
    ctx_id = lax.axis_index("ctx")
    dp_id = lax.axis_index("dp")
    groups, kv_here, ctx_dev, width = cache.shape
    total = kept.shape[2]
    prompts = assign.shape[0]
    slots = jnp.arange(prompts, dtype=jnp.int32)
    order = jnp.sum(jnp.where(assign[None, :] == slots[:, None], slots[None, :], 0), axis=1)
    edges = ctx_dev * jnp.arange(ctx_count + 1, dtype=jnp.int32)
    below = jnp.sum((kept[:, :, None, :] < edges[:, None]).astype(jnp.int32), axis=3)
    counts = below[:, :, 1:] - below[:, :, :-1]
    counts_mine, counts_theirs = halves_of(counts, dp_id, 1)
    query_mine, query_theirs = halves_of(queries[0], dp_id, 1)
    new_mine, new_theirs = halves_of(new_kv[0], dp_id, 1)
    counts_got, query_got, new_got = swapped((counts_theirs, query_theirs, new_theirs), "dp", 0)
    all_counts = in_dp_order(counts_mine, counts_got, dp_id, 0)
    query = in_dp_order(query_mine, query_got, dp_id, 0)
    new_rows = jnp.transpose(in_dp_order(new_mine, new_got, dp_id, 0), (1, 0, 2))
    is_here = (assign == ctx_id).astype(jnp.int32)
    slot_counts = jnp.sum(all_counts * is_here[:, None, None], axis=0)
    capacity = ctx_dev // 2
    offsets = jnp.arange(capacity, dtype=jnp.int32)
    bias = jnp.where(offsets < slot_counts[:, :, None], 0.0, neg_large).astype(jnp.float32)
    bias = bias.reshape(bias.shape[0], 1, ctx_count * capacity)
    return order, query, new_rows, bias


def local(cache, kept, assign, queries, new_kv, out_weight):
    groups, kv_here, ctx_dev, width = cache.shape
    if kv_here % 2:
        return local_by_rows(cache, kept, assign, queries, new_kv, out_weight)
    ctx_id = lax.axis_index("ctx")
    dp_id = lax.axis_index("dp")
    capacity = ctx_dev // 2
    per_group = queries.shape[2] // (kv_here * (width // 2))
    order, query, new_rows, bias = prepare(cache, kept, assign, queries, new_kv)
    picked = select_rows(
        cache.reshape(groups * kv_here, ctx_dev, width),
        kept.reshape(groups * kv_here, kept.shape[2]),
        ctx_id * ctx_dev,
        capacity,
    ).reshape(groups, kv_here, capacity, width)
    picked_mine, picked_theirs = halves_of(picked, dp_id, 1)
    picked_got = swapped(picked_theirs, "dp", 0)
    buffer = arrange(picked_mine, picked_got, order, dp_id)
    received = lax.all_to_all(buffer, "ctx", split_axis=0, concat_axis=0, tiled=True)
    head_out = attend_heads(query, received, bias, new_rows, per_group)
    out_mine, out_theirs = halves_of(head_out, dp_id, 0)
    out_got = swapped(out_theirs, "dp", 0)
    own_rows = in_dp_order(out_mine, out_got, dp_id, 1)
    gathered = lax.all_gather(own_rows, "ctx", axis=0)
    partials = project(gathered, out_weight, assign)
    return lax.psum_scatter(partials, "tensor", scatter_dimension=0, tiled=True)


def solution(mesh):
    placed = (
        P("dp", "tensor", "ctx", None),
        P("dp", "tensor", None),
        P(),
        P("ctx", "dp", "tensor"),
        P("ctx", "dp", "tensor", None),
        P("tensor", "ctx"),
    )
    return jax.shard_map(
        local, mesh=mesh, in_specs=placed, out_specs=P("tensor", "dp", "ctx"), check_vma=False
    )
```

```python
import functools
import math

import jax
import jax.numpy as jnp
from jax import lax
from jax.experimental import pallas as pl
from jax.experimental.pallas import tpu as pltpu
from jax.sharding import PartitionSpec as P

neg_large = -1e30
MESH = pl.DeviceIdType.MESH


def swapped(array, axis, distance):
    return lax.ppermute(array, axis, [(i, i ^ 1 << distance) for i in range(lax.axis_size(axis))])


def slot_prompt(assign, slot_id):
    matches = (assign == slot_id).astype(jnp.int32)
    return jnp.sum(matches * jnp.arange(assign.shape[0], dtype=jnp.int32))


def block_rows_of(flat_cache, kept_lists, block_start, first_rank, row_count, stride, capacity):
    offsets = jnp.arange(capacity, dtype=jnp.int32)
    rank_ids = jnp.clip(first_rank[:, None] + stride * offsets[None, :], 0, kept_lists.shape[1] - 1)
    places = jnp.take_along_axis(kept_lists, rank_ids, axis=1) - block_start
    is_valid = offsets[None, :] < row_count[:, None]
    spots = jnp.arange(flat_cache.shape[1], dtype=jnp.int32)
    chooser = ((places[:, :, None] == spots[None, None, :]) & is_valid[:, :, None]).astype(
        flat_cache.dtype
    )
    picked = jnp.einsum("gcq,gqw->gcw", chooser, flat_cache, preferred_element_type=jnp.float32)
    return picked.astype(flat_cache.dtype)


def padded_layout(rows, marks):
    senders, kv_here, capacity, row_width = rows.shape
    flat_rows = jnp.transpose(rows, (1, 0, 2, 3)).reshape(kv_here, senders * capacity, row_width)
    flat_marks = jnp.transpose(marks, (1, 0, 2)).reshape(kv_here, senders * capacity)
    return (flat_rows, flat_marks)


def attend_rows(query, row_start, kept_rows, kept_marks, new_rows, new_start):
    head_dim = kept_rows.shape[2] // 2
    score_scale = head_dim ** (-0.5)
    kept_scores = (
        jnp.einsum(
            "rkgd,knd->rkgn", query, kept_rows[:, :, :head_dim], preferred_element_type=jnp.float32
        )
        * score_scale
    )
    kept_scores = jnp.where((kept_marks > 0.5)[None, :, None, :], kept_scores, neg_large)
    new_scores = (
        jnp.einsum(
            "rkgd,nkd->rkgn", query, new_rows[:, :, :head_dim], preferred_element_type=jnp.float32
        )
        * score_scale
    )
    row_ids = row_start + jnp.arange(query.shape[0], dtype=jnp.int32)
    key_ids = new_start + jnp.arange(new_rows.shape[0], dtype=jnp.int32)
    visible = (key_ids[None, :] <= row_ids[:, None])[:, None, None, :]
    new_scores = jnp.where(visible, new_scores, neg_large)
    row_top = jnp.maximum(jnp.max(kept_scores, axis=3), jnp.max(new_scores, axis=3))
    kept_weights = jnp.exp(kept_scores - row_top[..., None])
    new_weights = jnp.exp(new_scores - row_top[..., None])
    weight_sum = jnp.sum(kept_weights, axis=3) + jnp.sum(new_weights, axis=3)
    weighted = jnp.einsum(
        "rkgn,knd->rkgd",
        kept_weights.astype(jnp.bfloat16),
        kept_rows[:, :, head_dim:],
        preferred_element_type=jnp.float32,
    )
    weighted = weighted + jnp.einsum(
        "rkgn,nkd->rkgd",
        new_weights.astype(jnp.bfloat16),
        new_rows[:, :, head_dim:],
        preferred_element_type=jnp.float32,
    )
    return (row_top, weight_sum, weighted)


def attend(query, row_start, kept_rows, kept_marks, new_rows, new_start):
    half_rows = query.shape[0] // 2
    first = attend_rows(query[:half_rows], row_start, kept_rows, kept_marks, new_rows, new_start)
    second = attend_rows(
        query[half_rows:], row_start + half_rows, kept_rows, kept_marks, new_rows, new_start
    )
    return tuple((jnp.concatenate([first[index], second[index]], axis=0) for index in range(3)))


def local_by_rows(cache, kept, assign, queries, new_kv, out_weight):
    ctx_count = lax.axis_size("ctx")
    ctx_id = lax.axis_index("ctx")
    dp_id = lax.axis_index("dp")
    groups, kv_here, ctx_dev, row_width = cache.shape
    head_dim = row_width // 2
    keep_total = kept.shape[2]
    flat_cache = cache.reshape(groups * kv_here, ctx_dev, row_width)
    kept_lists = kept.reshape(groups * kv_here, keep_total)
    block_start = ctx_id * ctx_dev
    rank_low = jnp.sum((kept_lists < block_start).astype(jnp.int32), axis=1)
    rank_high = jnp.sum((kept_lists < block_start + ctx_dev).astype(jnp.int32), axis=1)
    slot_ids = lax.dynamic_slice_in_dim(assign, dp_id * groups, groups)
    prompt = slot_prompt(assign, ctx_id)
    capacity = ctx_dev // 2
    row_count = rank_high - rank_low
    picked = block_rows_of(flat_cache, kept_lists, block_start, rank_low, row_count, 1, capacity)
    picked = picked.reshape(groups, kv_here, capacity, row_width)
    buffer = (
        jnp.zeros((ctx_count, kv_here, capacity, row_width), cache.dtype).at[slot_ids].set(picked)
    )
    counts = (
        jnp.zeros((ctx_count, kv_here), jnp.int32)
        .at[slot_ids]
        .set(row_count.reshape(groups, kv_here))
    )
    received, got_counts = (
        lax.all_to_all(buffer, "ctx", split_axis=0, concat_axis=0, tiled=True),
        lax.all_to_all(counts, "ctx", split_axis=0, concat_axis=0, tiled=True),
    )
    halves = received.reshape(ctx_count, kv_here, capacity // 2, 2, row_width)
    offsets = jnp.arange(capacity // 2, dtype=jnp.int32)
    even_marks = (2 * offsets[None, None, :] < got_counts[:, :, None]).astype(cache.dtype)
    odd_marks = (2 * offsets[None, None, :] + 1 < got_counts[:, :, None]).astype(cache.dtype)
    own_rows = jnp.where(dp_id == 0, halves[:, :, :, 0], halves[:, :, :, 1])
    own_marks = jnp.where(dp_id == 0, even_marks, odd_marks)
    their_rows = jnp.where(dp_id == 0, halves[:, :, :, 1], halves[:, :, :, 0])
    their_marks = jnp.where(dp_id == 0, odd_marks, even_marks)
    own_flat, own_flat_marks = padded_layout(own_rows, own_marks)
    their_flat, their_flat_marks = padded_layout(their_rows, their_marks)
    from_partner, partner_marks = swapped((their_flat, their_flat_marks), "dp", 0)
    owner_here = prompt // groups == dp_id
    kept_half = jnp.where(owner_here, own_flat, from_partner)
    kept_marks = jnp.where(owner_here, own_flat_marks, partner_marks)
    rows_here = queries.shape[1]
    per_group = queries.shape[2] // (kv_here * head_dim)
    own_query = queries[0].reshape(rows_here, kv_here, per_group, head_dim)
    own_new = new_kv[0]
    own_start = dp_id * rows_here
    other_kept, other_marks, other_new = swapped((kept_half, kept_marks, own_new), "dp", 0)
    all_kept = jnp.concatenate([kept_half, other_kept], axis=1)
    all_marks = jnp.concatenate([kept_marks, other_marks], axis=1)
    all_new = jnp.where(
        dp_id == 0,
        jnp.concatenate([own_new, other_new], axis=0),
        jnp.concatenate([other_new, own_new], axis=0),
    )
    row_top, weight_sum, weighted = attend(own_query, own_start, all_kept, all_marks, all_new, 0)
    head_out = (
        (weighted / weight_sum[..., None])
        .reshape(rows_here, kv_here * per_group * head_dim)
        .astype(jnp.bfloat16)
    )
    partials = jnp.dot(
        lax.all_gather(head_out, "ctx", axis=0, tiled=True),
        out_weight,
        preferred_element_type=jnp.float32,
    )
    partials = partials.reshape(ctx_count, rows_here, partials.shape[1])[assign]
    return lax.psum_scatter(
        partials.astype(jnp.bfloat16), "tensor", scatter_dimension=0, tiled=True
    )


def select_kernel(start_ref, kept_ref, cache_ref, out_ref):
    start = start_ref[0]
    kept = kept_ref[0]
    total = kept.shape[1]
    spots = cache_ref.shape[1]
    capacity = out_ref.shape[1]
    first = jnp.sum((kept < start).astype(jnp.int32))
    wide = jnp.broadcast_to(kept, (8, total))
    places = pltpu.roll(wide, lax.rem(total - first, total), 1)[:1, :capacity] - start
    spot_ids = lax.broadcasted_iota(jnp.int32, (spots, capacity), 0)
    chooser = (spot_ids == places).astype(jnp.float32).astype(jnp.bfloat16)
    picked = lax.dot_general(
        chooser, cache_ref[0], (((0,), (0,)), ((), ())), preferred_element_type=jnp.float32
    )
    out_ref[0] = picked.astype(out_ref.dtype)


def select_rows(flat_cache, kept_lists, block_start, capacity):
    lists, spots, width = flat_cache.shape
    total = kept_lists.shape[1]
    return pl.pallas_call(
        select_kernel,
        out_shape=jax.ShapeDtypeStruct((lists, capacity, width), flat_cache.dtype),
        grid_spec=pltpu.PrefetchScalarGridSpec(
            num_scalar_prefetch=1,
            grid=(lists,),
            in_specs=[
                pl.BlockSpec((1, 1, total), lambda i, s: (i, 0, 0)),
                pl.BlockSpec((1, spots, width), lambda i, s: (i, 0, 0)),
            ],
            out_specs=pl.BlockSpec((1, capacity, width), lambda i, s: (i, 0, 0)),
        ),
    )(block_start.reshape(1), kept_lists.reshape(lists, 1, total), flat_cache)


def arrange_kernel(groups, order_ref, dp_ref, mine_ref, got_ref, out_ref):
    from_mine = order_ref[pl.program_id(0)] // groups == dp_ref[0]

    @pl.when(from_mine)
    def _():
        out_ref[...] = mine_ref[...]

    @pl.when(jnp.logical_not(from_mine))
    def _():
        out_ref[...] = got_ref[...]


def arrange(mine, got, order, dp_id):
    groups, heads, capacity, width = mine.shape
    block = (1, heads, capacity, width)

    def source(i, order_ref, dp_ref):
        return (order_ref[i] % groups, 0, 0, 0)

    return pl.pallas_call(
        functools.partial(arrange_kernel, groups),
        out_shape=jax.ShapeDtypeStruct((order.shape[0], heads, capacity, width), mine.dtype),
        grid_spec=pltpu.PrefetchScalarGridSpec(
            num_scalar_prefetch=2,
            grid=(order.shape[0],),
            in_specs=[pl.BlockSpec(block, source), pl.BlockSpec(block, source)],
            out_specs=pl.BlockSpec(block, lambda i, a, b: (i, 0, 0, 0)),
        ),
    )(order, dp_id.reshape(1), mine, got)


def attend_kernel(q_ref, rows_ref, bias_ref, new_ref, out_ref):
    blocks, _, capacity, width = rows_ref.shape
    hd = width // 2
    rows = q_ref.shape[0]
    q = jnp.concatenate([q_ref[:, :hd], q_ref[:, hd:]], axis=0)
    keys = rows_ref[:, 0, :, :hd].reshape(blocks * capacity, hd)
    values = rows_ref[:, 0, :, hd:].reshape(blocks * capacity, hd)
    new_keys = new_ref[0, :, :hd]
    new_values = new_ref[0, :, hd:]
    scale = hd**-0.5 * math.log2(math.e)
    dims = (((1,), (1,)), ((), ()))
    kept_scores = lax.dot_general(q, keys, dims, preferred_element_type=jnp.float32) * scale
    kept_scores = kept_scores + bias_ref[0]
    new_scores = lax.dot_general(q, new_keys, dims, preferred_element_type=jnp.float32) * scale
    row_ids = lax.rem(lax.broadcasted_iota(jnp.int32, new_scores.shape, 0), rows)
    key_ids = lax.broadcasted_iota(jnp.int32, new_scores.shape, 1)
    new_scores = jnp.where(key_ids <= row_ids, new_scores, neg_large)
    top = jnp.maximum(
        jnp.max(kept_scores, axis=1, keepdims=True), jnp.max(new_scores, axis=1, keepdims=True)
    )
    kept_weights = jnp.exp2(kept_scores - top)
    new_weights = jnp.exp2(new_scores - top)
    total = jnp.sum(kept_weights, axis=1, keepdims=True) + jnp.sum(new_weights, axis=1, keepdims=True)
    weighted = jnp.dot(
        kept_weights.astype(jnp.bfloat16), values, preferred_element_type=jnp.float32
    ) + jnp.dot(new_weights.astype(jnp.bfloat16), new_values, preferred_element_type=jnp.float32)
    result = (weighted / total).astype(out_ref.dtype)
    out_ref[:, :hd] = result[:rows]
    out_ref[:, hd:] = result[rows:]


def attend_heads(query, received, bias, new_rows, per_group):
    rows, columns = query.shape
    blocks, heads, capacity, width = received.shape
    hd = width // 2
    pairs = per_group // 2
    return pl.pallas_call(
        attend_kernel,
        out_shape=jax.ShapeDtypeStruct(query.shape, query.dtype),
        grid=(heads, pairs),
        in_specs=[
            pl.BlockSpec((rows, 2 * hd), lambda h, j: (0, h * pairs + j)),
            pl.BlockSpec((blocks, 1, capacity, width), lambda h, j: (0, h, 0, 0)),
            pl.BlockSpec((1, 1, blocks * capacity), lambda h, j: (h, 0, 0)),
            pl.BlockSpec((1, rows, width), lambda h, j: (h, 0, 0)),
        ],
        out_specs=pl.BlockSpec((rows, 2 * hd), lambda h, j: (0, h * pairs + j)),
        compiler_params=pltpu.CompilerParams(vmem_limit_bytes=48 * 1024 * 1024),
    )(query, received, bias, new_rows)


def gather_project_kernel(
    assign_ref, heads_ref, weight_hbm, out_ref,
    gat, weight, part, send_buf, recv_buf,
    send, recv, y_send, core_send, core_recv, weight_sem,
):
    c = lax.axis_index("ctx")
    t = lax.axis_index("tensor")
    d = lax.axis_index("dp")
    z, x = c // 2, c % 2
    zs = gat.shape[1] // 2
    rows = gat.shape[2]
    tile = part.shape[3]
    partner_x = z * 2 + 1 - x
    kept = out_ref.shape[0]

    load_weight = pltpu.make_async_copy(weight_hbm, weight, weight_sem)
    load_weight.start()
    barrier = pltpu.get_barrier_semaphore()
    for target in ({"ctx": partner_x}, {"dp": 1 - d}, {"tensor": 1 - t}):
        pl.semaphore_signal(barrier, inc=1, device_id=target, device_id_type=MESH)

    @pl.when(z > 0)
    def _():
        pl.semaphore_signal(barrier, inc=1, device_id={"ctx": c - 2}, device_id_type=MESH)

    @pl.when(z < zs - 1)
    def _():
        pl.semaphore_signal(barrier, inc=1, device_id={"ctx": c + 2}, device_id_type=MESH)

    pl.semaphore_wait(barrier, 3 + (z > 0).astype(jnp.int32) + (z < zs - 1).astype(jnp.int32))

    cols = (d, 1 - d)

    def copy(piece, slot, channel):
        ref = gat.at[cols[piece], slot]
        target = (c + 2, c - 2, partner_x)[channel]
        return pltpu.make_async_remote_copy(
            src_ref=ref, dst_ref=ref, send_sem=send.at[piece, slot, channel],
            recv_sem=recv.at[piece, slot], device_id={"ctx": target}, device_id_type=MESH,
        )

    def up(piece, slot):
        @pl.when(z < zs - 1)
        def _():
            copy(piece, slot, 0).start()

    def down(piece, slot):
        @pl.when(z > 0)
        def _():
            copy(piece, slot, 1).start()

    def arrived(piece, slot):
        copy(piece, slot, 2).wait_recv()

    y_copy = pltpu.make_async_remote_copy(
        src_ref=heads_ref.at[pl.ds((1 - d) * rows, rows)], dst_ref=gat.at[d, c],
        send_sem=y_send, recv_sem=recv.at[1, c], device_id={"dp": 1 - d}, device_id_type=MESH,
    )
    y_copy.start()
    gat[d, c] = heads_ref[pl.ds(pl.multiple_of(d * rows, rows), rows)]
    up(0, c)
    down(0, c)
    copy(0, c, 2).start()
    arrived(1, c)
    copy(1, c, 2).start()
    up(1, c)
    down(1, c)
    arrived(1, partner_x)
    up(1, partner_x)
    down(1, partner_x)
    for k in range(1, zs):
        @pl.when(z >= k)
        def _():
            arrived(0, c - 2 * k)
            up(0, c - 2 * k)
            copy(0, c - 2 * k, 2).start()

        @pl.when(z + k < zs)
        def _():
            arrived(0, c + 2 * k)
            down(0, c + 2 * k)
            copy(0, c + 2 * k, 2).start()

        for base in (c, partner_x):
            @pl.when(z >= k)
            def _():
                arrived(1, base - 2 * k)
                up(1, base - 2 * k)

            @pl.when(z + k < zs)
            def _():
                arrived(1, base + 2 * k)
                down(1, base + 2 * k)

    for zo in range(zs):
        arrived(0, zo * 2 + 1 - x)
    load_weight.wait()

    slots = gat.shape[1]
    depth = gat.shape[3]
    tiles = part.shape[0]

    def exchange(n):
        return pltpu.make_async_remote_copy(
            src_ref=send_buf.at[n], dst_ref=recv_buf.at[n], send_sem=core_send.at[n],
            recv_sem=core_recv.at[n], device_id={"tensor": 1 - t}, device_id_type=MESH,
        )

    def tile_step(n, carry):
        span = pl.ds(pl.multiple_of(n * tile, tile), tile)
        product = jnp.dot(
            gat[0].reshape(slots * rows, depth), weight[:depth, span], preferred_element_type=jnp.float32
        ) + jnp.dot(
            gat[1].reshape(slots * rows, depth), weight[depth:, span], preferred_element_type=jnp.float32
        )
        part[n] = product.reshape(slots, rows, tile)
        for j in range(kept):
            send_buf[n, j] = part[n, assign_ref[(1 - t) * kept + j]].astype(send_buf.dtype)
        exchange(n).start()
        return carry

    lax.fori_loop(0, tiles, tile_step, 0)
    for n in range(tiles):
        exchange(n).wait_recv()
        for j in range(kept):
            total = part[n, assign_ref[t * kept + j]] + recv_buf[n, j].astype(jnp.float32)
            out_ref[j, :, n * tile : (n + 1) * tile] = total.astype(out_ref.dtype)

    y_copy.wait_send()
    for n in range(tiles):
        exchange(n).wait_send()
    copy(0, c, 2).wait_send()
    copy(1, c, 2).wait_send()

    @pl.when(z < zs - 1)
    def _():
        copy(0, c, 0).wait_send()
        copy(1, c, 0).wait_send()
        copy(1, partner_x, 0).wait_send()

    @pl.when(z > 0)
    def _():
        copy(0, c, 1).wait_send()
        copy(1, c, 1).wait_send()
        copy(1, partner_x, 1).wait_send()

    for k in range(1, zs):
        @pl.when(z >= k)
        def _():
            copy(0, c - 2 * k, 2).wait_send()

            @pl.when(z < zs - 1)
            def _():
                copy(0, c - 2 * k, 0).wait_send()
                copy(1, c - 2 * k, 0).wait_send()
                copy(1, partner_x - 2 * k, 0).wait_send()

        @pl.when(z + k < zs)
        def _():
            copy(0, c + 2 * k, 2).wait_send()

            @pl.when(z > 0)
            def _():
                copy(0, c + 2 * k, 1).wait_send()
                copy(1, c + 2 * k, 1).wait_send()
                copy(1, partner_x + 2 * k, 1).wait_send()


def gather_project(head_out, out_weight, assign):
    slots = assign.shape[0]
    rows, half_depth = head_out.shape[0] // 2, head_out.shape[1]
    depth, columns = out_weight.shape
    kept = slots // 2
    tile = 256
    tiles = columns // tile
    kind = head_out.dtype
    dma = pltpu.SemaphoreType.DMA
    return pl.pallas_call(
        gather_project_kernel,
        out_shape=jax.ShapeDtypeStruct((kept, rows, columns), kind),
        in_specs=[
            pl.BlockSpec(memory_space=pltpu.SMEM),
            pl.BlockSpec(memory_space=pltpu.VMEM),
            pl.BlockSpec(memory_space=pl.ANY),
        ],
        out_specs=pl.BlockSpec(memory_space=pltpu.VMEM),
        scratch_shapes=[
            pltpu.VMEM((2, slots, rows, half_depth), kind),
            pltpu.VMEM((depth, columns), kind),
            pltpu.VMEM((tiles, slots, rows, tile), jnp.float32),
            pltpu.VMEM((tiles, kept, rows, tile), kind),
            pltpu.VMEM((tiles, kept, rows, tile), kind),
            dma((2, slots, 3)),
            dma((2, slots)),
            dma,
            dma((tiles,)),
            dma((tiles,)),
            dma,
        ],
        compiler_params=pltpu.CompilerParams(
            collective_id=1, has_side_effects=True, vmem_limit_bytes=48 * 1024 * 1024
        ),
    )(assign, head_out, out_weight)


def in_dp_order(own, other, dp_id, axis):
    return jnp.where(
        dp_id == 0,
        jnp.concatenate([own, other], axis=axis),
        jnp.concatenate([other, own], axis=axis),
    )


def halves_of(array, dp_id, axis):
    size = array.shape[axis] // 2
    mine = lax.dynamic_slice_in_dim(array, dp_id * size, size, axis)
    theirs = lax.dynamic_slice_in_dim(array, (1 - dp_id) * size, size, axis)
    return mine, theirs


def prepare(cache, kept, assign, queries, new_kv):
    ctx_count = lax.axis_size("ctx")
    ctx_id = lax.axis_index("ctx")
    dp_id = lax.axis_index("dp")
    groups, kv_here, ctx_dev, width = cache.shape
    total = kept.shape[2]
    prompts = assign.shape[0]
    slots = jnp.arange(prompts, dtype=jnp.int32)
    order = jnp.sum(jnp.where(assign[None, :] == slots[:, None], slots[None, :], 0), axis=1)
    edges = ctx_dev * jnp.arange(ctx_count + 1, dtype=jnp.int32)
    below = jnp.sum((kept[:, :, None, :] < edges[:, None]).astype(jnp.int32), axis=3)
    counts = below[:, :, 1:] - below[:, :, :-1]
    counts_mine, counts_theirs = halves_of(counts, dp_id, 1)
    query_mine, query_theirs = halves_of(queries[0], dp_id, 1)
    new_mine, new_theirs = halves_of(new_kv[0], dp_id, 1)
    counts_got, query_got, new_got = swapped((counts_theirs, query_theirs, new_theirs), "dp", 0)
    all_counts = in_dp_order(counts_mine, counts_got, dp_id, 0)
    query = in_dp_order(query_mine, query_got, dp_id, 0)
    new_rows = jnp.transpose(in_dp_order(new_mine, new_got, dp_id, 0), (1, 0, 2))
    is_here = (assign == ctx_id).astype(jnp.int32)
    slot_counts = jnp.sum(all_counts * is_here[:, None, None], axis=0)
    capacity = ctx_dev // 2
    offsets = jnp.arange(capacity, dtype=jnp.int32)
    bias = jnp.where(offsets < slot_counts[:, :, None], 0.0, neg_large).astype(jnp.float32)
    bias = bias.reshape(bias.shape[0], 1, ctx_count * capacity)
    return order, query, new_rows, bias


def local(cache, kept, assign, queries, new_kv, out_weight):
    groups, kv_here, ctx_dev, width = cache.shape
    if kv_here % 2 or lax.axis_size("ctx") != 8 or lax.axis_size("tensor") != 2:
        return local_by_rows(cache, kept, assign, queries, new_kv, out_weight)
    ctx_id = lax.axis_index("ctx")
    dp_id = lax.axis_index("dp")
    capacity = ctx_dev // 2
    per_group = queries.shape[2] // (kv_here * (width // 2))
    order, query, new_rows, bias = prepare(cache, kept, assign, queries, new_kv)
    picked = select_rows(
        cache.reshape(groups * kv_here, ctx_dev, width),
        kept.reshape(groups * kv_here, kept.shape[2]),
        ctx_id * ctx_dev,
        capacity,
    ).reshape(groups, kv_here, capacity, width)
    picked_mine, picked_theirs = halves_of(picked, dp_id, 1)
    picked_got = swapped(picked_theirs, "dp", 0)
    buffer = arrange(picked_mine, picked_got, order, dp_id)
    received = lax.all_to_all(buffer, "ctx", split_axis=0, concat_axis=0, tiled=True)
    head_out = attend_heads(query, received, bias, new_rows, per_group)
    return gather_project(head_out, out_weight, assign)


def solution(mesh):
    placed = (
        P("dp", "tensor", "ctx", None),
        P("dp", "tensor", None),
        P(),
        P("ctx", "dp", "tensor"),
        P("ctx", "dp", "tensor", None),
        P("tensor", "ctx"),
    )
    return jax.shard_map(
        local, mesh=mesh, in_specs=placed, out_specs=P("tensor", "dp", "ctx"), check_vma=False
    )
```

```python
import functools
import math

import jax
import jax.numpy as jnp
from jax import lax
from jax.experimental import pallas as pl
from jax.experimental.pallas import tpu as pltpu
from jax.sharding import PartitionSpec as P

neg_large = -1e30
MESH = pl.DeviceIdType.MESH


def swapped(array, axis, distance):
    return lax.ppermute(array, axis, [(i, i ^ 1 << distance) for i in range(lax.axis_size(axis))])


def slot_prompt(assign, slot_id):
    matches = (assign == slot_id).astype(jnp.int32)
    return jnp.sum(matches * jnp.arange(assign.shape[0], dtype=jnp.int32))


def block_rows_of(flat_cache, kept_lists, block_start, first_rank, row_count, stride, capacity):
    offsets = jnp.arange(capacity, dtype=jnp.int32)
    rank_ids = jnp.clip(first_rank[:, None] + stride * offsets[None, :], 0, kept_lists.shape[1] - 1)
    places = jnp.take_along_axis(kept_lists, rank_ids, axis=1) - block_start
    is_valid = offsets[None, :] < row_count[:, None]
    spots = jnp.arange(flat_cache.shape[1], dtype=jnp.int32)
    chooser = ((places[:, :, None] == spots[None, None, :]) & is_valid[:, :, None]).astype(
        flat_cache.dtype
    )
    picked = jnp.einsum("gcq,gqw->gcw", chooser, flat_cache, preferred_element_type=jnp.float32)
    return picked.astype(flat_cache.dtype)


def padded_layout(rows, marks):
    senders, kv_here, capacity, row_width = rows.shape
    flat_rows = jnp.transpose(rows, (1, 0, 2, 3)).reshape(kv_here, senders * capacity, row_width)
    flat_marks = jnp.transpose(marks, (1, 0, 2)).reshape(kv_here, senders * capacity)
    return (flat_rows, flat_marks)


def attend_rows(query, row_start, kept_rows, kept_marks, new_rows, new_start):
    head_dim = kept_rows.shape[2] // 2
    score_scale = head_dim ** (-0.5)
    kept_scores = (
        jnp.einsum(
            "rkgd,knd->rkgn", query, kept_rows[:, :, :head_dim], preferred_element_type=jnp.float32
        )
        * score_scale
    )
    kept_scores = jnp.where((kept_marks > 0.5)[None, :, None, :], kept_scores, neg_large)
    new_scores = (
        jnp.einsum(
            "rkgd,nkd->rkgn", query, new_rows[:, :, :head_dim], preferred_element_type=jnp.float32
        )
        * score_scale
    )
    row_ids = row_start + jnp.arange(query.shape[0], dtype=jnp.int32)
    key_ids = new_start + jnp.arange(new_rows.shape[0], dtype=jnp.int32)
    visible = (key_ids[None, :] <= row_ids[:, None])[:, None, None, :]
    new_scores = jnp.where(visible, new_scores, neg_large)
    row_top = jnp.maximum(jnp.max(kept_scores, axis=3), jnp.max(new_scores, axis=3))
    kept_weights = jnp.exp(kept_scores - row_top[..., None])
    new_weights = jnp.exp(new_scores - row_top[..., None])
    weight_sum = jnp.sum(kept_weights, axis=3) + jnp.sum(new_weights, axis=3)
    weighted = jnp.einsum(
        "rkgn,knd->rkgd",
        kept_weights.astype(jnp.bfloat16),
        kept_rows[:, :, head_dim:],
        preferred_element_type=jnp.float32,
    )
    weighted = weighted + jnp.einsum(
        "rkgn,nkd->rkgd",
        new_weights.astype(jnp.bfloat16),
        new_rows[:, :, head_dim:],
        preferred_element_type=jnp.float32,
    )
    return (row_top, weight_sum, weighted)


def attend(query, row_start, kept_rows, kept_marks, new_rows, new_start):
    half_rows = query.shape[0] // 2
    first = attend_rows(query[:half_rows], row_start, kept_rows, kept_marks, new_rows, new_start)
    second = attend_rows(
        query[half_rows:], row_start + half_rows, kept_rows, kept_marks, new_rows, new_start
    )
    return tuple((jnp.concatenate([first[index], second[index]], axis=0) for index in range(3)))


def local_by_rows(cache, kept, assign, queries, new_kv, out_weight):
    ctx_count = lax.axis_size("ctx")
    ctx_id = lax.axis_index("ctx")
    dp_id = lax.axis_index("dp")
    groups, kv_here, ctx_dev, row_width = cache.shape
    head_dim = row_width // 2
    keep_total = kept.shape[2]
    flat_cache = cache.reshape(groups * kv_here, ctx_dev, row_width)
    kept_lists = kept.reshape(groups * kv_here, keep_total)
    block_start = ctx_id * ctx_dev
    rank_low = jnp.sum((kept_lists < block_start).astype(jnp.int32), axis=1)
    rank_high = jnp.sum((kept_lists < block_start + ctx_dev).astype(jnp.int32), axis=1)
    slot_ids = lax.dynamic_slice_in_dim(assign, dp_id * groups, groups)
    prompt = slot_prompt(assign, ctx_id)
    capacity = ctx_dev // 2
    row_count = rank_high - rank_low
    picked = block_rows_of(flat_cache, kept_lists, block_start, rank_low, row_count, 1, capacity)
    picked = picked.reshape(groups, kv_here, capacity, row_width)
    buffer = (
        jnp.zeros((ctx_count, kv_here, capacity, row_width), cache.dtype).at[slot_ids].set(picked)
    )
    counts = (
        jnp.zeros((ctx_count, kv_here), jnp.int32)
        .at[slot_ids]
        .set(row_count.reshape(groups, kv_here))
    )
    received, got_counts = (
        lax.all_to_all(buffer, "ctx", split_axis=0, concat_axis=0, tiled=True),
        lax.all_to_all(counts, "ctx", split_axis=0, concat_axis=0, tiled=True),
    )
    halves = received.reshape(ctx_count, kv_here, capacity // 2, 2, row_width)
    offsets = jnp.arange(capacity // 2, dtype=jnp.int32)
    even_marks = (2 * offsets[None, None, :] < got_counts[:, :, None]).astype(cache.dtype)
    odd_marks = (2 * offsets[None, None, :] + 1 < got_counts[:, :, None]).astype(cache.dtype)
    own_rows = jnp.where(dp_id == 0, halves[:, :, :, 0], halves[:, :, :, 1])
    own_marks = jnp.where(dp_id == 0, even_marks, odd_marks)
    their_rows = jnp.where(dp_id == 0, halves[:, :, :, 1], halves[:, :, :, 0])
    their_marks = jnp.where(dp_id == 0, odd_marks, even_marks)
    own_flat, own_flat_marks = padded_layout(own_rows, own_marks)
    their_flat, their_flat_marks = padded_layout(their_rows, their_marks)
    from_partner, partner_marks = swapped((their_flat, their_flat_marks), "dp", 0)
    owner_here = prompt // groups == dp_id
    kept_half = jnp.where(owner_here, own_flat, from_partner)
    kept_marks = jnp.where(owner_here, own_flat_marks, partner_marks)
    rows_here = queries.shape[1]
    per_group = queries.shape[2] // (kv_here * head_dim)
    own_query = queries[0].reshape(rows_here, kv_here, per_group, head_dim)
    own_new = new_kv[0]
    own_start = dp_id * rows_here
    other_kept, other_marks, other_new = swapped((kept_half, kept_marks, own_new), "dp", 0)
    all_kept = jnp.concatenate([kept_half, other_kept], axis=1)
    all_marks = jnp.concatenate([kept_marks, other_marks], axis=1)
    all_new = jnp.where(
        dp_id == 0,
        jnp.concatenate([own_new, other_new], axis=0),
        jnp.concatenate([other_new, own_new], axis=0),
    )
    row_top, weight_sum, weighted = attend(own_query, own_start, all_kept, all_marks, all_new, 0)
    head_out = (
        (weighted / weight_sum[..., None])
        .reshape(rows_here, kv_here * per_group * head_dim)
        .astype(jnp.bfloat16)
    )
    partials = jnp.dot(
        lax.all_gather(head_out, "ctx", axis=0, tiled=True),
        out_weight,
        preferred_element_type=jnp.float32,
    )
    partials = partials.reshape(ctx_count, rows_here, partials.shape[1])[assign]
    return lax.psum_scatter(
        partials.astype(jnp.bfloat16), "tensor", scatter_dimension=0, tiled=True
    )


def places_kernel(start_ref, kept_ref, out_ref):
    start = start_ref[0]
    lists, total = kept_ref.shape
    capacity = out_ref.shape[2]
    for i in range(lists):
        kept = kept_ref[i : i + 1]
        first = jnp.sum((kept < start).astype(jnp.int32))
        wide = jnp.broadcast_to(kept, (8, total))
        rolled = pltpu.roll(wide, lax.rem(total - first, total), 1)
        out_ref[i] = rolled[:1, :capacity] - start


def places_of(kept_lists, block_start, capacity):
    return pl.pallas_call(
        places_kernel,
        out_shape=jax.ShapeDtypeStruct((kept_lists.shape[0], 1, capacity), jnp.int32),
        in_specs=[
            pl.BlockSpec(memory_space=pltpu.SMEM),
            pl.BlockSpec(memory_space=pltpu.VMEM),
        ],
        out_specs=pl.BlockSpec(memory_space=pltpu.VMEM),
    )(block_start.reshape(1), kept_lists)


def relayout_kernel(
    order_ref, places_ref, cache_hbm, out_ref,
    cache, stage, outgoing, load_sem, y_send, y_recv, ctx_send, ctx_recv, *pool
):
    c = lax.axis_index("ctx")
    d = lax.axis_index("dp")
    groups = stage.shape[1]
    slots = out_ref.shape[0]
    kv_here = cache_hbm.shape[0] // groups
    heads = kv_here // 2
    capacity, width = places_ref.shape[2], cache.shape[2]
    piece = stage.shape[2]
    pieces = capacity // piece

    def load(i):
        return pltpu.make_async_copy(cache_hbm.at[i], cache.at[i], load_sem.at[i])

    for j in range(heads):
        for side in (1 - d, d):
            for g in range(groups):
                load(g * kv_here + side * heads + j).start()

    barrier = pltpu.get_barrier_semaphore()
    pl.semaphore_signal(barrier, inc=1, device_id={"dp": 1 - d}, device_id_type=MESH)
    for k in range(1, slots):
        pl.semaphore_signal(
            barrier, inc=1, device_id={"ctx": lax.rem(c + k, slots)}, device_id_type=MESH
        )
    pl.semaphore_wait(barrier, slots)

    spot_ids = lax.broadcasted_iota(jnp.int32, (cache.shape[1], capacity), 0)

    def pick(i):
        load(i).wait()
        chooser = (spot_ids == places_ref[i]).astype(jnp.float32).astype(jnp.bfloat16)
        return lax.dot_general(
            chooser, cache[i], (((0,), (0,)), ((), ())), preferred_element_type=jnp.float32
        ).astype(cache.dtype)

    def y_copy(q, g, sender):
        return pltpu.make_async_remote_copy(
            src_ref=stage.at[q, g], dst_ref=pool[q].at[sender * groups + g], send_sem=y_send.at[q, g],
            recv_sem=y_recv.at[q, g], device_id={"dp": 1 - d}, device_id_type=MESH,
        )

    def ctx_copy(q, k):
        span = pl.ds((q % pieces) * piece, piece)
        return pltpu.make_async_remote_copy(
            src_ref=outgoing.at[q, k - 1], dst_ref=out_ref.at[c, q // pieces, span],
            send_sem=ctx_send.at[q, k - 1], recv_sem=ctx_recv.at[q, k - 1],
            device_id={"ctx": lax.rem(c + k, slots)}, device_id_type=MESH,
        )

    def pick_theirs(j):
        def step(g, carry):
            picked = pick(g * kv_here + (1 - d) * heads + j)
            for half in range(pieces):
                stage[j * pieces + half, g] = picked[half * piece : (half + 1) * piece]
            y_copy(j * pieces, g, d).start()
            return carry

        lax.fori_loop(0, groups, step, 0)
        for half in range(1, pieces):
            for g in range(groups):
                y_copy(j * pieces + half, g, d).start()

    def pick_mine(j):
        def step(g, carry):
            picked = pick(g * kv_here + d * heads + j)
            for half in range(pieces):
                pool[j * pieces + half][d * groups + g] = picked[half * piece : (half + 1) * piece]
            return carry

        lax.fori_loop(0, groups, step, 0)

    def scatter(q):
        for g in range(groups):
            y_copy(q, g, 1 - d).wait_recv()
        for k in (4, 5, 3, 2, 6, 1, 7) if slots == 8 else range(1, slots):
            outgoing[q, k - 1] = pool[q][order_ref[lax.rem(c + k, slots)]]
            ctx_copy(q, k).start()
        start = (q % pieces) * piece
        out_ref[c, q // pieces, start : start + piece] = pool[q][order_ref[c]]

    pick_theirs(0)
    pick_mine(0)
    for j in range(heads):
        if j + 1 < heads:
            pick_theirs(j + 1)
        for half in range(pieces):
            scatter(j * pieces + half)
            if half == 0 and j + 1 < heads:
                pick_mine(j + 1)

    for q in range(heads * pieces):
        for k in range(1, slots):
            sender = lax.rem(c + slots - k, slots)
            start = (q % pieces) * piece
            pltpu.make_async_remote_copy(
                src_ref=outgoing.at[q, k - 1],
                dst_ref=out_ref.at[sender, q // pieces, pl.ds(start, piece)],
                send_sem=ctx_send.at[q, k - 1], recv_sem=ctx_recv.at[q, k - 1],
                device_id={"ctx": lax.rem(c + k, slots)}, device_id_type=MESH,
            ).wait()
        for g in range(groups):
            y_copy(q, g, d).wait_send()


def relayout(flat_cache, places, order, groups):
    lists, spots, width = flat_cache.shape
    capacity = places.shape[2]
    slots = order.shape[0]
    heads = lists // groups // 2
    pieces = 2
    piece = capacity // pieces
    kind = flat_cache.dtype
    dma = pltpu.SemaphoreType.DMA
    return pl.pallas_call(
        relayout_kernel,
        out_shape=jax.ShapeDtypeStruct((slots, heads, capacity, width), kind),
        in_specs=[
            pl.BlockSpec(memory_space=pltpu.SMEM),
            pl.BlockSpec(memory_space=pltpu.VMEM),
            pl.BlockSpec(memory_space=pl.ANY),
        ],
        out_specs=pl.BlockSpec(memory_space=pltpu.VMEM),
        scratch_shapes=[
            pltpu.VMEM((lists, spots, width), kind),
            pltpu.VMEM((heads * pieces, groups, piece, width), kind),
            pltpu.VMEM((heads * pieces, slots - 1, piece, width), kind),
            dma((lists,)),
            dma((heads * pieces, groups)),
            dma((heads * pieces, groups)),
            dma((heads * pieces, slots - 1)),
            dma((heads * pieces, slots - 1)),
        ]
        + [pltpu.VMEM((2 * groups, piece, width), kind)] * (heads * pieces),
        cost_estimate=pl.CostEstimate(flops=int(3e10), bytes_accessed=int(1.5e8), transcendentals=0),
        compiler_params=pltpu.CompilerParams(
            collective_id=0, has_side_effects=True, vmem_limit_bytes=48 * 1024 * 1024
        ),
    )(order, places, flat_cache)


def attend_kernel(q_ref, rows_ref, bias_ref, new_ref, out_ref):
    blocks, _, capacity, width = rows_ref.shape
    hd = width // 2
    rows = q_ref.shape[0]
    q = jnp.concatenate([q_ref[:, :hd], q_ref[:, hd:]], axis=0)
    keys = rows_ref[:, 0, :, :hd].reshape(blocks * capacity, hd)
    values = rows_ref[:, 0, :, hd:].reshape(blocks * capacity, hd)
    new_keys = new_ref[0, :, :hd]
    new_values = new_ref[0, :, hd:]
    scale = hd**-0.5 * math.log2(math.e)
    dims = (((1,), (1,)), ((), ()))
    kept_scores = lax.dot_general(q, keys, dims, preferred_element_type=jnp.float32) * scale
    kept_scores = kept_scores + bias_ref[0]
    new_scores = lax.dot_general(q, new_keys, dims, preferred_element_type=jnp.float32) * scale
    row_ids = lax.rem(lax.broadcasted_iota(jnp.int32, new_scores.shape, 0), rows)
    key_ids = lax.broadcasted_iota(jnp.int32, new_scores.shape, 1)
    new_scores = jnp.where(key_ids <= row_ids, new_scores, neg_large)
    top = jnp.maximum(
        jnp.max(kept_scores, axis=1, keepdims=True), jnp.max(new_scores, axis=1, keepdims=True)
    )
    kept_weights = jnp.exp2(kept_scores - top)
    new_weights = jnp.exp2(new_scores - top)
    total = jnp.sum(kept_weights, axis=1, keepdims=True) + jnp.sum(new_weights, axis=1, keepdims=True)
    weighted = jnp.dot(
        kept_weights.astype(jnp.bfloat16), values, preferred_element_type=jnp.float32
    ) + jnp.dot(new_weights.astype(jnp.bfloat16), new_values, preferred_element_type=jnp.float32)
    result = (weighted / total).astype(out_ref.dtype)
    out_ref[:, :hd] = result[:rows]
    out_ref[:, hd:] = result[rows:]


def attend_heads(query, received, bias, new_rows, per_group):
    rows, columns = query.shape
    blocks, heads, capacity, width = received.shape
    hd = width // 2
    pairs = per_group // 2
    return pl.pallas_call(
        attend_kernel,
        out_shape=jax.ShapeDtypeStruct(query.shape, query.dtype),
        grid=(heads, pairs),
        in_specs=[
            pl.BlockSpec((rows, 2 * hd), lambda h, j: (0, h * pairs + j)),
            pl.BlockSpec((blocks, 1, capacity, width), lambda h, j: (0, h, 0, 0)),
            pl.BlockSpec((1, 1, blocks * capacity), lambda h, j: (h, 0, 0)),
            pl.BlockSpec((1, rows, width), lambda h, j: (h, 0, 0)),
        ],
        out_specs=pl.BlockSpec((rows, 2 * hd), lambda h, j: (0, h * pairs + j)),
        compiler_params=pltpu.CompilerParams(vmem_limit_bytes=48 * 1024 * 1024),
    )(query, received, bias, new_rows)


def gather_project_kernel(
    assign_ref, heads_ref, weight_hbm, out_ref,
    gat, weight, part, send_buf, recv_buf,
    send, recv, y_send, core_send, core_recv, weight_sem,
):
    c = lax.axis_index("ctx")
    t = lax.axis_index("tensor")
    d = lax.axis_index("dp")
    z, x = c // 2, c % 2
    zs = gat.shape[1] // 2
    rows = gat.shape[2]
    tile = part.shape[3]
    partner_x = z * 2 + 1 - x
    kept = out_ref.shape[0]

    load_weight = pltpu.make_async_copy(weight_hbm, weight, weight_sem)
    load_weight.start()
    barrier = pltpu.get_barrier_semaphore()
    for target in ({"ctx": partner_x}, {"dp": 1 - d}, {"tensor": 1 - t}):
        pl.semaphore_signal(barrier, inc=1, device_id=target, device_id_type=MESH)

    @pl.when(z > 0)
    def _():
        pl.semaphore_signal(barrier, inc=1, device_id={"ctx": c - 2}, device_id_type=MESH)

    @pl.when(z < zs - 1)
    def _():
        pl.semaphore_signal(barrier, inc=1, device_id={"ctx": c + 2}, device_id_type=MESH)

    pl.semaphore_wait(barrier, 3 + (z > 0).astype(jnp.int32) + (z < zs - 1).astype(jnp.int32))

    cols = (d, 1 - d)

    def copy(piece, slot, channel):
        ref = gat.at[cols[piece], slot]
        target = (c + 2, c - 2, partner_x)[channel]
        return pltpu.make_async_remote_copy(
            src_ref=ref, dst_ref=ref, send_sem=send.at[piece, slot, channel],
            recv_sem=recv.at[piece, slot], device_id={"ctx": target}, device_id_type=MESH,
        )

    def up(piece, slot):
        @pl.when(z < zs - 1)
        def _():
            copy(piece, slot, 0).start()

    def down(piece, slot):
        @pl.when(z > 0)
        def _():
            copy(piece, slot, 1).start()

    def arrived(piece, slot):
        copy(piece, slot, 2).wait_recv()

    y_copy = pltpu.make_async_remote_copy(
        src_ref=heads_ref.at[pl.ds((1 - d) * rows, rows)], dst_ref=gat.at[d, c],
        send_sem=y_send, recv_sem=recv.at[1, c], device_id={"dp": 1 - d}, device_id_type=MESH,
    )
    y_copy.start()
    gat[d, c] = heads_ref[pl.ds(pl.multiple_of(d * rows, rows), rows)]
    up(0, c)
    down(0, c)
    copy(0, c, 2).start()
    arrived(1, c)
    copy(1, c, 2).start()
    up(1, c)
    down(1, c)
    arrived(1, partner_x)
    up(1, partner_x)
    down(1, partner_x)
    for k in range(1, zs):
        @pl.when(z >= k)
        def _():
            arrived(0, c - 2 * k)
            up(0, c - 2 * k)
            copy(0, c - 2 * k, 2).start()

        @pl.when(z + k < zs)
        def _():
            arrived(0, c + 2 * k)
            down(0, c + 2 * k)
            copy(0, c + 2 * k, 2).start()

        for base in (c, partner_x):
            @pl.when(z >= k)
            def _():
                arrived(1, base - 2 * k)
                up(1, base - 2 * k)

            @pl.when(z + k < zs)
            def _():
                arrived(1, base + 2 * k)
                down(1, base + 2 * k)

    for zo in range(zs):
        arrived(0, zo * 2 + 1 - x)
    load_weight.wait()

    slots = gat.shape[1]
    depth = gat.shape[3]
    tiles = part.shape[0]

    def exchange(n):
        return pltpu.make_async_remote_copy(
            src_ref=send_buf.at[n], dst_ref=recv_buf.at[n], send_sem=core_send.at[n],
            recv_sem=core_recv.at[n], device_id={"tensor": 1 - t}, device_id_type=MESH,
        )

    def tile_step(n, carry):
        span = pl.ds(pl.multiple_of(n * tile, tile), tile)
        product = jnp.dot(
            gat[0].reshape(slots * rows, depth), weight[:depth, span], preferred_element_type=jnp.float32
        ) + jnp.dot(
            gat[1].reshape(slots * rows, depth), weight[depth:, span], preferred_element_type=jnp.float32
        )
        part[n] = product.reshape(slots, rows, tile)
        for j in range(kept):
            send_buf[n, j] = part[n, assign_ref[(1 - t) * kept + j]].astype(send_buf.dtype)
        exchange(n).start()
        return carry

    lax.fori_loop(0, tiles, tile_step, 0)
    for n in range(tiles):
        exchange(n).wait_recv()
        for j in range(kept):
            total = part[n, assign_ref[t * kept + j]] + recv_buf[n, j].astype(jnp.float32)
            out_ref[j, :, n * tile : (n + 1) * tile] = total.astype(out_ref.dtype)

    y_copy.wait_send()
    for n in range(tiles):
        exchange(n).wait_send()
    copy(0, c, 2).wait_send()
    copy(1, c, 2).wait_send()

    @pl.when(z < zs - 1)
    def _():
        copy(0, c, 0).wait_send()
        copy(1, c, 0).wait_send()
        copy(1, partner_x, 0).wait_send()

    @pl.when(z > 0)
    def _():
        copy(0, c, 1).wait_send()
        copy(1, c, 1).wait_send()
        copy(1, partner_x, 1).wait_send()

    for k in range(1, zs):
        @pl.when(z >= k)
        def _():
            copy(0, c - 2 * k, 2).wait_send()

            @pl.when(z < zs - 1)
            def _():
                copy(0, c - 2 * k, 0).wait_send()
                copy(1, c - 2 * k, 0).wait_send()
                copy(1, partner_x - 2 * k, 0).wait_send()

        @pl.when(z + k < zs)
        def _():
            copy(0, c + 2 * k, 2).wait_send()

            @pl.when(z > 0)
            def _():
                copy(0, c + 2 * k, 1).wait_send()
                copy(1, c + 2 * k, 1).wait_send()
                copy(1, partner_x + 2 * k, 1).wait_send()


def gather_project(head_out, out_weight, assign):
    slots = assign.shape[0]
    rows, half_depth = head_out.shape[0] // 2, head_out.shape[1]
    depth, columns = out_weight.shape
    kept = slots // 2
    tile = 256
    tiles = columns // tile
    kind = head_out.dtype
    dma = pltpu.SemaphoreType.DMA
    return pl.pallas_call(
        gather_project_kernel,
        out_shape=jax.ShapeDtypeStruct((kept, rows, columns), kind),
        in_specs=[
            pl.BlockSpec(memory_space=pltpu.SMEM),
            pl.BlockSpec(memory_space=pltpu.VMEM),
            pl.BlockSpec(memory_space=pl.ANY),
        ],
        out_specs=pl.BlockSpec(memory_space=pltpu.VMEM),
        scratch_shapes=[
            pltpu.VMEM((2, slots, rows, half_depth), kind),
            pltpu.VMEM((depth, columns), kind),
            pltpu.VMEM((tiles, slots, rows, tile), jnp.float32),
            pltpu.VMEM((tiles, kept, rows, tile), kind),
            pltpu.VMEM((tiles, kept, rows, tile), kind),
            dma((2, slots, 3)),
            dma((2, slots)),
            dma,
            dma((tiles,)),
            dma((tiles,)),
            dma,
        ],
        compiler_params=pltpu.CompilerParams(
            collective_id=1, has_side_effects=True, vmem_limit_bytes=48 * 1024 * 1024
        ),
    )(assign, head_out, out_weight)


def in_dp_order(own, other, dp_id, axis):
    return jnp.where(
        dp_id == 0,
        jnp.concatenate([own, other], axis=axis),
        jnp.concatenate([other, own], axis=axis),
    )


def halves_of(array, dp_id, axis):
    size = array.shape[axis] // 2
    mine = lax.dynamic_slice_in_dim(array, dp_id * size, size, axis)
    theirs = lax.dynamic_slice_in_dim(array, (1 - dp_id) * size, size, axis)
    return mine, theirs


def prepare(cache, kept, assign, queries, new_kv):
    ctx_count = lax.axis_size("ctx")
    ctx_id = lax.axis_index("ctx")
    dp_id = lax.axis_index("dp")
    groups, kv_here, ctx_dev, width = cache.shape
    total = kept.shape[2]
    prompts = assign.shape[0]
    slots = jnp.arange(prompts, dtype=jnp.int32)
    order = jnp.sum(jnp.where(assign[None, :] == slots[:, None], slots[None, :], 0), axis=1)
    edges = ctx_dev * jnp.arange(ctx_count + 1, dtype=jnp.int32)
    below = jnp.sum((kept[:, :, None, :] < edges[:, None]).astype(jnp.int32), axis=3)
    counts = below[:, :, 1:] - below[:, :, :-1]
    counts_mine, counts_theirs = halves_of(counts, dp_id, 1)
    query_mine, query_theirs = halves_of(queries[0], dp_id, 1)
    new_mine, new_theirs = halves_of(new_kv[0], dp_id, 1)
    counts_got, query_got, new_got = swapped((counts_theirs, query_theirs, new_theirs), "dp", 0)
    all_counts = in_dp_order(counts_mine, counts_got, dp_id, 0)
    query = in_dp_order(query_mine, query_got, dp_id, 0)
    new_rows = jnp.transpose(in_dp_order(new_mine, new_got, dp_id, 0), (1, 0, 2))
    is_here = (assign == ctx_id).astype(jnp.int32)
    slot_counts = jnp.sum(all_counts * is_here[:, None, None], axis=0)
    capacity = ctx_dev // 2
    offsets = jnp.arange(capacity, dtype=jnp.int32)
    bias = jnp.where(offsets < slot_counts[:, :, None], 0.0, neg_large).astype(jnp.float32)
    bias = bias.reshape(bias.shape[0], 1, ctx_count * capacity)
    return order, query, new_rows, bias


def local(cache, kept, assign, queries, new_kv, out_weight):
    groups, kv_here, ctx_dev, width = cache.shape
    if kv_here % 2 or lax.axis_size("ctx") != 8 or lax.axis_size("tensor") != 2:
        return local_by_rows(cache, kept, assign, queries, new_kv, out_weight)
    ctx_id = lax.axis_index("ctx")
    capacity = ctx_dev // 2
    per_group = queries.shape[2] // (kv_here * (width // 2))
    order, query, new_rows, bias = prepare(cache, kept, assign, queries, new_kv)
    places = places_of(
        kept.reshape(groups * kv_here, kept.shape[2]), ctx_id * ctx_dev, capacity
    )
    flat_cache = cache.reshape(groups * kv_here, ctx_dev, width)
    received = relayout(flat_cache, places, order, groups)
    head_out = attend_heads(query, received, bias, new_rows, per_group)
    return gather_project(head_out, out_weight, assign)


def solution(mesh):
    placed = (
        P("dp", "tensor", "ctx", None),
        P("dp", "tensor", None),
        P(),
        P("ctx", "dp", "tensor"),
        P("ctx", "dp", "tensor", None),
        P("tensor", "ctx"),
    )
    return jax.shard_map(
        local, mesh=mesh, in_specs=placed, out_specs=P("tensor", "dp", "ctx"), check_vma=False
    )
```

```python
import functools
import math

import jax
import jax.numpy as jnp
from jax import lax
from jax.experimental import pallas as pl
from jax.experimental.pallas import tpu as pltpu
from jax.sharding import PartitionSpec as P

neg_large = -1e30
MESH = pl.DeviceIdType.MESH


def swapped(array, axis, distance):
    return lax.ppermute(array, axis, [(i, i ^ 1 << distance) for i in range(lax.axis_size(axis))])


def slot_prompt(assign, slot_id):
    matches = (assign == slot_id).astype(jnp.int32)
    return jnp.sum(matches * jnp.arange(assign.shape[0], dtype=jnp.int32))


def block_rows_of(flat_cache, kept_lists, block_start, first_rank, row_count, stride, capacity):
    offsets = jnp.arange(capacity, dtype=jnp.int32)
    rank_ids = jnp.clip(first_rank[:, None] + stride * offsets[None, :], 0, kept_lists.shape[1] - 1)
    places = jnp.take_along_axis(kept_lists, rank_ids, axis=1) - block_start
    is_valid = offsets[None, :] < row_count[:, None]
    spots = jnp.arange(flat_cache.shape[1], dtype=jnp.int32)
    chooser = ((places[:, :, None] == spots[None, None, :]) & is_valid[:, :, None]).astype(
        flat_cache.dtype
    )
    picked = jnp.einsum("gcq,gqw->gcw", chooser, flat_cache, preferred_element_type=jnp.float32)
    return picked.astype(flat_cache.dtype)


def padded_layout(rows, marks):
    senders, kv_here, capacity, row_width = rows.shape
    flat_rows = jnp.transpose(rows, (1, 0, 2, 3)).reshape(kv_here, senders * capacity, row_width)
    flat_marks = jnp.transpose(marks, (1, 0, 2)).reshape(kv_here, senders * capacity)
    return (flat_rows, flat_marks)


def attend_rows(query, row_start, kept_rows, kept_marks, new_rows, new_start):
    head_dim = kept_rows.shape[2] // 2
    score_scale = head_dim ** (-0.5)
    kept_scores = (
        jnp.einsum(
            "rkgd,knd->rkgn", query, kept_rows[:, :, :head_dim], preferred_element_type=jnp.float32
        )
        * score_scale
    )
    kept_scores = jnp.where((kept_marks > 0.5)[None, :, None, :], kept_scores, neg_large)
    new_scores = (
        jnp.einsum(
            "rkgd,nkd->rkgn", query, new_rows[:, :, :head_dim], preferred_element_type=jnp.float32
        )
        * score_scale
    )
    row_ids = row_start + jnp.arange(query.shape[0], dtype=jnp.int32)
    key_ids = new_start + jnp.arange(new_rows.shape[0], dtype=jnp.int32)
    visible = (key_ids[None, :] <= row_ids[:, None])[:, None, None, :]
    new_scores = jnp.where(visible, new_scores, neg_large)
    row_top = jnp.maximum(jnp.max(kept_scores, axis=3), jnp.max(new_scores, axis=3))
    kept_weights = jnp.exp(kept_scores - row_top[..., None])
    new_weights = jnp.exp(new_scores - row_top[..., None])
    weight_sum = jnp.sum(kept_weights, axis=3) + jnp.sum(new_weights, axis=3)
    weighted = jnp.einsum(
        "rkgn,knd->rkgd",
        kept_weights.astype(jnp.bfloat16),
        kept_rows[:, :, head_dim:],
        preferred_element_type=jnp.float32,
    )
    weighted = weighted + jnp.einsum(
        "rkgn,nkd->rkgd",
        new_weights.astype(jnp.bfloat16),
        new_rows[:, :, head_dim:],
        preferred_element_type=jnp.float32,
    )
    return (row_top, weight_sum, weighted)


def attend(query, row_start, kept_rows, kept_marks, new_rows, new_start):
    half_rows = query.shape[0] // 2
    first = attend_rows(query[:half_rows], row_start, kept_rows, kept_marks, new_rows, new_start)
    second = attend_rows(
        query[half_rows:], row_start + half_rows, kept_rows, kept_marks, new_rows, new_start
    )
    return tuple((jnp.concatenate([first[index], second[index]], axis=0) for index in range(3)))


def local_by_rows(cache, kept, assign, queries, new_kv, out_weight):
    ctx_count = lax.axis_size("ctx")
    ctx_id = lax.axis_index("ctx")
    dp_id = lax.axis_index("dp")
    groups, kv_here, ctx_dev, row_width = cache.shape
    head_dim = row_width // 2
    keep_total = kept.shape[2]
    flat_cache = cache.reshape(groups * kv_here, ctx_dev, row_width)
    kept_lists = kept.reshape(groups * kv_here, keep_total)
    block_start = ctx_id * ctx_dev
    rank_low = jnp.sum((kept_lists < block_start).astype(jnp.int32), axis=1)
    rank_high = jnp.sum((kept_lists < block_start + ctx_dev).astype(jnp.int32), axis=1)
    slot_ids = lax.dynamic_slice_in_dim(assign, dp_id * groups, groups)
    prompt = slot_prompt(assign, ctx_id)
    capacity = ctx_dev // 2
    row_count = rank_high - rank_low
    picked = block_rows_of(flat_cache, kept_lists, block_start, rank_low, row_count, 1, capacity)
    picked = picked.reshape(groups, kv_here, capacity, row_width)
    buffer = (
        jnp.zeros((ctx_count, kv_here, capacity, row_width), cache.dtype).at[slot_ids].set(picked)
    )
    counts = (
        jnp.zeros((ctx_count, kv_here), jnp.int32)
        .at[slot_ids]
        .set(row_count.reshape(groups, kv_here))
    )
    received, got_counts = (
        lax.all_to_all(buffer, "ctx", split_axis=0, concat_axis=0, tiled=True),
        lax.all_to_all(counts, "ctx", split_axis=0, concat_axis=0, tiled=True),
    )
    halves = received.reshape(ctx_count, kv_here, capacity // 2, 2, row_width)
    offsets = jnp.arange(capacity // 2, dtype=jnp.int32)
    even_marks = (2 * offsets[None, None, :] < got_counts[:, :, None]).astype(cache.dtype)
    odd_marks = (2 * offsets[None, None, :] + 1 < got_counts[:, :, None]).astype(cache.dtype)
    own_rows = jnp.where(dp_id == 0, halves[:, :, :, 0], halves[:, :, :, 1])
    own_marks = jnp.where(dp_id == 0, even_marks, odd_marks)
    their_rows = jnp.where(dp_id == 0, halves[:, :, :, 1], halves[:, :, :, 0])
    their_marks = jnp.where(dp_id == 0, odd_marks, even_marks)
    own_flat, own_flat_marks = padded_layout(own_rows, own_marks)
    their_flat, their_flat_marks = padded_layout(their_rows, their_marks)
    from_partner, partner_marks = swapped((their_flat, their_flat_marks), "dp", 0)
    owner_here = prompt // groups == dp_id
    kept_half = jnp.where(owner_here, own_flat, from_partner)
    kept_marks = jnp.where(owner_here, own_flat_marks, partner_marks)
    rows_here = queries.shape[1]
    per_group = queries.shape[2] // (kv_here * head_dim)
    own_query = queries[0].reshape(rows_here, kv_here, per_group, head_dim)
    own_new = new_kv[0]
    own_start = dp_id * rows_here
    other_kept, other_marks, other_new = swapped((kept_half, kept_marks, own_new), "dp", 0)
    all_kept = jnp.concatenate([kept_half, other_kept], axis=1)
    all_marks = jnp.concatenate([kept_marks, other_marks], axis=1)
    all_new = jnp.where(
        dp_id == 0,
        jnp.concatenate([own_new, other_new], axis=0),
        jnp.concatenate([other_new, own_new], axis=0),
    )
    row_top, weight_sum, weighted = attend(own_query, own_start, all_kept, all_marks, all_new, 0)
    head_out = (
        (weighted / weight_sum[..., None])
        .reshape(rows_here, kv_here * per_group * head_dim)
        .astype(jnp.bfloat16)
    )
    partials = jnp.dot(
        lax.all_gather(head_out, "ctx", axis=0, tiled=True),
        out_weight,
        preferred_element_type=jnp.float32,
    )
    partials = partials.reshape(ctx_count, rows_here, partials.shape[1])[assign]
    return lax.psum_scatter(
        partials.astype(jnp.bfloat16), "tensor", scatter_dimension=0, tiled=True
    )


def places_kernel(start_ref, kept_ref, out_ref):
    start = start_ref[0]
    lists, total = kept_ref.shape
    capacity = out_ref.shape[2]
    for i in range(lists):
        kept = kept_ref[i : i + 1]
        first = jnp.sum((kept < start).astype(jnp.int32))
        wide = jnp.broadcast_to(kept, (8, total))
        rolled = pltpu.roll(wide, lax.rem(total - first, total), 1)
        out_ref[i] = rolled[:1, :capacity] - start


def places_of(kept_lists, block_start, capacity):
    return pl.pallas_call(
        places_kernel,
        out_shape=jax.ShapeDtypeStruct((kept_lists.shape[0], 1, capacity), jnp.int32),
        in_specs=[
            pl.BlockSpec(memory_space=pltpu.SMEM),
            pl.BlockSpec(memory_space=pltpu.VMEM),
        ],
        out_specs=pl.BlockSpec(memory_space=pltpu.VMEM),
    )(block_start.reshape(1), kept_lists)


def relayout_kernel(
    order_ref, places_ref, cache_hbm, query_hbm, new_hbm, bias_hbm, head_out_ref,
    out_ref, query, new_rows, bias, cache, stage, outgoing,
    load_sem, y_send, y_recv, ctx_send, ctx_recv, side_send, side_recv, side_own, *pool
):
    c = lax.axis_index("ctx")
    d = lax.axis_index("dp")
    groups = stage.shape[1]
    slots = out_ref.shape[0]
    kv_here = cache_hbm.shape[0] // groups
    heads = kv_here // 2
    capacity, width = places_ref.shape[2], cache.shape[2]
    piece = stage.shape[2]
    pieces = capacity // piece

    def load(i):
        return pltpu.make_async_copy(cache_hbm.at[i], cache.at[i], load_sem.at[i])

    for j in range(heads):
        for side in (1 - d, d):
            for g in range(groups):
                load(g * kv_here + side * heads + j).start()

    barrier = pltpu.get_barrier_semaphore()
    pl.semaphore_signal(barrier, inc=1, device_id={"dp": 1 - d}, device_id_type=MESH)
    for k in range(1, slots):
        pl.semaphore_signal(
            barrier, inc=1, device_id={"ctx": lax.rem(c + k, slots)}, device_id_type=MESH
        )
    pl.semaphore_wait(barrier, slots)

    rows, columns = query_hbm.shape[0], query.shape[1]

    def side_parts(side, place):
        across = pl.ds(pl.multiple_of(side * columns, columns), columns)
        down = pl.ds(pl.multiple_of(place * rows, rows), rows)
        return (
            (query_hbm.at[:, across], query.at[down]),
            (new_hbm.at[side], new_rows.at[:, down]),
            (bias_hbm.at[side], bias.at[pl.ds(place * groups, groups)]),
        )

    def side_sends(place):
        return [
            pltpu.make_async_remote_copy(
                src_ref=source, dst_ref=target, send_sem=side_send.at[i], recv_sem=side_recv.at[i],
                device_id={"dp": 1 - d}, device_id_type=MESH,
            )
            for i, (source, target) in enumerate(side_parts(1 - d, place))
        ]

    own_parts = [
        pltpu.make_async_copy(source, target, side_own.at[i])
        for i, (source, target) in enumerate(side_parts(d, d))
    ]
    for part in own_parts:
        part.start()

    spot_ids = lax.broadcasted_iota(jnp.int32, (cache.shape[1], capacity), 0)

    def pick(i):
        load(i).wait()
        chooser = (spot_ids == places_ref[i]).astype(jnp.float32).astype(jnp.bfloat16)
        return lax.dot_general(
            chooser, cache[i], (((0,), (0,)), ((), ())), preferred_element_type=jnp.float32
        ).astype(cache.dtype)

    def y_copy(q, g, sender):
        return pltpu.make_async_remote_copy(
            src_ref=stage.at[q, g], dst_ref=pool[q].at[sender * groups + g], send_sem=y_send.at[q, g],
            recv_sem=y_recv.at[q, g], device_id={"dp": 1 - d}, device_id_type=MESH,
        )

    def ctx_copy(q, k):
        span = pl.ds((q % pieces) * piece, piece)
        return pltpu.make_async_remote_copy(
            src_ref=outgoing.at[q, k - 1], dst_ref=out_ref.at[c, q // pieces, span],
            send_sem=ctx_send.at[q, k - 1], recv_sem=ctx_recv.at[q, k - 1],
            device_id={"ctx": lax.rem(c + k, slots)}, device_id_type=MESH,
        )

    def pick_theirs(j):
        def step(g, carry):
            picked = pick(g * kv_here + (1 - d) * heads + j)
            for half in range(pieces):
                stage[j * pieces + half, g] = picked[half * piece : (half + 1) * piece]
            y_copy(j * pieces, g, d).start()
            return carry

        lax.fori_loop(0, groups, step, 0)
        for half in range(1, pieces):
            for g in range(groups):
                y_copy(j * pieces + half, g, d).start()

    def pick_mine(j):
        def step(g, carry):
            picked = pick(g * kv_here + d * heads + j)
            for half in range(pieces):
                pool[j * pieces + half][d * groups + g] = picked[half * piece : (half + 1) * piece]
            return carry

        lax.fori_loop(0, groups, step, 0)

    def scatter(q):
        for g in range(groups):
            y_copy(q, g, 1 - d).wait_recv()
        for k in (4, 5, 3, 2, 6, 1, 7) if slots == 8 else range(1, slots):
            outgoing[q, k - 1] = pool[q][order_ref[lax.rem(c + k, slots)]]
            ctx_copy(q, k).start()
        start = (q % pieces) * piece
        out_ref[c, q // pieces, start : start + piece] = pool[q][order_ref[c]]

    pick_theirs(0)
    pick_mine(0)
    for j in range(heads):
        if j + 1 < heads:
            pick_theirs(j + 1)
        for half in range(pieces):
            scatter(j * pieces + half)
            if half == 0 and j + 1 < heads:
                pick_mine(j + 1)
            if half == 0 and j == 0:
                for part in side_sends(d):
                    part.start()

    def finish(q):
        for k in range(1, slots):
            sender = lax.rem(c + slots - k, slots)
            start = (q % pieces) * piece
            pltpu.make_async_remote_copy(
                src_ref=outgoing.at[q, k - 1],
                dst_ref=out_ref.at[sender, q // pieces, pl.ds(start, piece)],
                send_sem=ctx_send.at[q, k - 1], recv_sem=ctx_recv.at[q, k - 1],
                device_id={"ctx": lax.rem(c + k, slots)}, device_id_type=MESH,
            ).wait()
        for g in range(groups):
            y_copy(q, g, d).wait_send()

    hd = width // 2
    tiles = columns // heads // (2 * hd)
    for h in range(heads):
        for half in range(pieces):
            finish(h * pieces + half)
        if h == 0:
            for part in own_parts:
                part.wait()
            for part in side_sends(1 - d):
                part.wait_recv()

        def tile_step(n, carry):
            low = pl.multiple_of((h * tiles + n) * 2 * hd, 2 * hd)
            first, second = attend_tile(
                query[:, pl.ds(low, hd)], query[:, pl.ds(low + hd, hd)],
                out_ref[:, h], bias[order_ref[c], h : h + 1], new_rows[h],
            )
            head_out_ref[:, pl.ds(low, hd)] = first
            head_out_ref[:, pl.ds(low + hd, hd)] = second
            return carry

        lax.fori_loop(0, tiles, tile_step, 0)
    for part in side_sends(d):
        part.wait_send()


def relayout_attend(flat_cache, places, order, groups, queries, new_sides, bias_sides):
    lists, spots, width = flat_cache.shape
    capacity = places.shape[2]
    slots = order.shape[0]
    heads = lists // groups // 2
    pieces = 2
    piece = capacity // pieces
    kind = flat_cache.dtype
    rows, columns = queries.shape[0], queries.shape[1] // 2
    dma = pltpu.SemaphoreType.DMA
    return pl.pallas_call(
        relayout_kernel,
        out_shape=jax.ShapeDtypeStruct((2 * rows, columns), kind),
        in_specs=[
            pl.BlockSpec(memory_space=pltpu.SMEM),
            pl.BlockSpec(memory_space=pltpu.VMEM),
            pl.BlockSpec(memory_space=pl.ANY),
            pl.BlockSpec(memory_space=pl.ANY),
            pl.BlockSpec(memory_space=pltpu.VMEM),
            pl.BlockSpec(memory_space=pltpu.VMEM),
        ],
        out_specs=pl.BlockSpec(memory_space=pltpu.VMEM),
        scratch_shapes=[
            pltpu.VMEM((slots, heads, capacity, width), kind),
            pltpu.VMEM((2 * rows, columns), kind),
            pltpu.VMEM((heads, 2 * rows, width), kind),
            pltpu.VMEM((2 * groups,) + bias_sides.shape[2:], jnp.float32),
            pltpu.VMEM((lists, spots, width), kind),
            pltpu.VMEM((heads * pieces, groups, piece, width), kind),
            pltpu.VMEM((heads * pieces, slots - 1, piece, width), kind),
            dma((lists,)),
            dma((heads * pieces, groups)),
            dma((heads * pieces, groups)),
            dma((heads * pieces, slots - 1)),
            dma((heads * pieces, slots - 1)),
            dma((3,)),
            dma((3,)),
            dma((3,)),
        ]
        + [pltpu.VMEM((2 * groups, piece, width), kind)] * (heads * pieces),
        cost_estimate=pl.CostEstimate(flops=int(3e10), bytes_accessed=int(1.5e8), transcendentals=0),
        compiler_params=pltpu.CompilerParams(
            collective_id=0, has_side_effects=True, vmem_limit_bytes=48 * 1024 * 1024
        ),
    )(order, places, flat_cache, queries, new_sides, bias_sides)


def attend_tile(first_query, second_query, received, bias, new_rows):
    blocks, capacity, width = received.shape
    rows, hd = first_query.shape
    q = jnp.concatenate([first_query, second_query], axis=0)
    keys = received[:, :, :hd].reshape(blocks * capacity, hd)
    values = received[:, :, hd:].reshape(blocks * capacity, hd)
    new_keys = new_rows[:, :hd]
    new_values = new_rows[:, hd:]
    scale = hd**-0.5 * math.log2(math.e)
    dims = (((1,), (1,)), ((), ()))
    kept_scores = lax.dot_general(q, keys, dims, preferred_element_type=jnp.float32) * scale
    kept_scores = kept_scores + bias
    new_scores = lax.dot_general(q, new_keys, dims, preferred_element_type=jnp.float32) * scale
    row_ids = lax.rem(lax.broadcasted_iota(jnp.int32, new_scores.shape, 0), rows)
    key_ids = lax.broadcasted_iota(jnp.int32, new_scores.shape, 1)
    new_scores = jnp.where(key_ids <= row_ids, new_scores, neg_large)
    top = jnp.maximum(
        jnp.max(kept_scores, axis=1, keepdims=True), jnp.max(new_scores, axis=1, keepdims=True)
    )
    kept_weights = jnp.exp2(kept_scores - top)
    new_weights = jnp.exp2(new_scores - top)
    total = jnp.sum(kept_weights, axis=1, keepdims=True) + jnp.sum(new_weights, axis=1, keepdims=True)
    weighted = jnp.dot(
        kept_weights.astype(jnp.bfloat16), values, preferred_element_type=jnp.float32
    ) + jnp.dot(new_weights.astype(jnp.bfloat16), new_values, preferred_element_type=jnp.float32)
    result = (weighted / total).astype(first_query.dtype)
    return result[:rows], result[rows:]


def gather_project_kernel(
    assign_ref, heads_ref, weight_hbm, out_ref,
    gat, weight, part, send_buf, recv_buf,
    send, recv, y_send, core_send, core_recv, weight_sem,
):
    c = lax.axis_index("ctx")
    t = lax.axis_index("tensor")
    d = lax.axis_index("dp")
    z, x = c // 2, c % 2
    zs = gat.shape[1] // 2
    rows = gat.shape[2]
    tile = part.shape[3]
    partner_x = z * 2 + 1 - x
    kept = out_ref.shape[0]

    load_weight = pltpu.make_async_copy(weight_hbm, weight, weight_sem)
    load_weight.start()
    barrier = pltpu.get_barrier_semaphore()
    for target in ({"ctx": partner_x}, {"dp": 1 - d}, {"tensor": 1 - t}):
        pl.semaphore_signal(barrier, inc=1, device_id=target, device_id_type=MESH)

    @pl.when(z > 0)
    def _():
        pl.semaphore_signal(barrier, inc=1, device_id={"ctx": c - 2}, device_id_type=MESH)

    @pl.when(z < zs - 1)
    def _():
        pl.semaphore_signal(barrier, inc=1, device_id={"ctx": c + 2}, device_id_type=MESH)

    pl.semaphore_wait(barrier, 3 + (z > 0).astype(jnp.int32) + (z < zs - 1).astype(jnp.int32))

    cut = rows // 4
    spans = ((d, 0, cut), (d, cut, rows), (1 - d, 0, rows // 2), (1 - d, rows // 2, rows))
    x_first = (0,)
    z_first = (1, 2, 3)

    def copy(piece, slot, channel):
        col, low, high = spans[piece]
        ref = gat.at[col, slot, pl.ds(low, high - low)]
        target = (c + 2, c - 2, partner_x)[channel]
        return pltpu.make_async_remote_copy(
            src_ref=ref, dst_ref=ref, send_sem=send.at[piece, slot, channel],
            recv_sem=recv.at[piece, slot], device_id={"ctx": target}, device_id_type=MESH,
        )

    def up(piece, slot):
        @pl.when(z < zs - 1)
        def _():
            copy(piece, slot, 0).start()

    def down(piece, slot):
        @pl.when(z > 0)
        def _():
            copy(piece, slot, 1).start()

    def arrived(piece, slot):
        copy(piece, slot, 2).wait_recv()

    def y_copy(piece):
        _, low, high = spans[piece]
        return pltpu.make_async_remote_copy(
            src_ref=heads_ref.at[pl.ds(pl.multiple_of((1 - d) * rows + low, 16), high - low)],
            dst_ref=gat.at[d, c, pl.ds(low, high - low)],
            send_sem=y_send.at[piece - 2], recv_sem=recv.at[piece, c],
            device_id={"dp": 1 - d}, device_id_type=MESH,
        )

    y_copy(2).start()
    y_copy(3).start()
    gat[d, c] = heads_ref[pl.ds(pl.multiple_of(d * rows, rows), rows)]
    copy(0, c, 2).start()
    up(1, c)
    down(1, c)
    copy(1, c, 2).start()
    up(0, c)
    down(0, c)
    for piece in (2, 3):
        arrived(piece, c)
        up(piece, c)
        down(piece, c)
        copy(piece, c, 2).start()
    arrived(0, partner_x)
    up(0, partner_x)
    down(0, partner_x)
    for k in range(1, zs):
        for piece in (1, 0, 2, 3):
            for base in (c, partner_x) if piece in x_first else (c,):
                @pl.when(z >= k)
                def _():
                    arrived(piece, base - 2 * k)
                    up(piece, base - 2 * k)
                    if piece in z_first:
                        copy(piece, base - 2 * k, 2).start()

                @pl.when(z + k < zs)
                def _():
                    arrived(piece, base + 2 * k)
                    down(piece, base + 2 * k)
                    if piece in z_first:
                        copy(piece, base + 2 * k, 2).start()

    for piece in z_first:
        for zo in range(zs):
            arrived(piece, zo * 2 + 1 - x)
    load_weight.wait()

    slots = gat.shape[1]
    depth = gat.shape[3]
    tiles = part.shape[0]

    def exchange(n):
        return pltpu.make_async_remote_copy(
            src_ref=send_buf.at[n], dst_ref=recv_buf.at[n], send_sem=core_send.at[n],
            recv_sem=core_recv.at[n], device_id={"tensor": 1 - t}, device_id_type=MESH,
        )

    def tile_step(n, carry):
        span = pl.ds(pl.multiple_of(n * tile, tile), tile)
        product = jnp.dot(
            gat[0].reshape(slots * rows, depth), weight[:depth, span], preferred_element_type=jnp.float32
        ) + jnp.dot(
            gat[1].reshape(slots * rows, depth), weight[depth:, span], preferred_element_type=jnp.float32
        )
        part[n] = product.reshape(slots, rows, tile)
        for j in range(kept):
            send_buf[n, j] = part[n, assign_ref[(1 - t) * kept + j]].astype(send_buf.dtype)
        exchange(n).start()
        return carry

    lax.fori_loop(0, tiles, tile_step, 0)
    for n in range(tiles):
        exchange(n).wait_recv()
        for j in range(kept):
            total = part[n, assign_ref[t * kept + j]] + recv_buf[n, j].astype(jnp.float32)
            out_ref[j, :, n * tile : (n + 1) * tile] = total.astype(out_ref.dtype)

    y_copy(2).wait_send()
    y_copy(3).wait_send()
    for n in range(tiles):
        exchange(n).wait_send()
    for piece in x_first + z_first:
        copy(piece, c, 2).wait_send()
        for base in (c, partner_x) if piece in x_first else (c,):
            @pl.when(z < zs - 1)
            def _():
                copy(piece, base, 0).wait_send()

            @pl.when(z > 0)
            def _():
                copy(piece, base, 1).wait_send()

            for k in range(1, zs):
                @pl.when(z >= k)
                def _():
                    if piece in z_first:
                        copy(piece, base - 2 * k, 2).wait_send()

                    @pl.when(z < zs - 1)
                    def _():
                        copy(piece, base - 2 * k, 0).wait_send()

                @pl.when(z + k < zs)
                def _():
                    if piece in z_first:
                        copy(piece, base + 2 * k, 2).wait_send()

                    @pl.when(z > 0)
                    def _():
                        copy(piece, base + 2 * k, 1).wait_send()


def gather_project(head_out, out_weight, assign):
    slots = assign.shape[0]
    rows, half_depth = head_out.shape[0] // 2, head_out.shape[1]
    depth, columns = out_weight.shape
    kept = slots // 2
    tile = 256
    tiles = columns // tile
    kind = head_out.dtype
    dma = pltpu.SemaphoreType.DMA
    return pl.pallas_call(
        gather_project_kernel,
        out_shape=jax.ShapeDtypeStruct((kept, rows, columns), kind),
        in_specs=[
            pl.BlockSpec(memory_space=pltpu.SMEM),
            pl.BlockSpec(memory_space=pltpu.VMEM),
            pl.BlockSpec(memory_space=pl.ANY),
        ],
        out_specs=pl.BlockSpec(memory_space=pltpu.VMEM),
        scratch_shapes=[
            pltpu.VMEM((2, slots, rows, half_depth), kind),
            pltpu.VMEM((depth, columns), kind),
            pltpu.VMEM((tiles, slots, rows, tile), jnp.float32),
            pltpu.VMEM((tiles, kept, rows, tile), kind),
            pltpu.VMEM((tiles, kept, rows, tile), kind),
            dma((4, slots, 3)),
            dma((4, slots)),
            dma((2,)),
            dma((tiles,)),
            dma((tiles,)),
            dma,
        ],
        compiler_params=pltpu.CompilerParams(
            collective_id=1, has_side_effects=True, vmem_limit_bytes=48 * 1024 * 1024
        ),
    )(assign, head_out, out_weight)


def local(cache, kept, assign, queries, new_kv, out_weight):
    groups, kv_here, ctx_dev, width = cache.shape
    ctx_count = lax.axis_size("ctx")
    if kv_here % 2 or ctx_count != 8 or lax.axis_size("tensor") != 2:
        return local_by_rows(cache, kept, assign, queries, new_kv, out_weight)
    ctx_id = lax.axis_index("ctx")
    capacity = ctx_dev // 2
    heads = kv_here // 2
    rows = queries.shape[1]
    slots = jnp.arange(assign.shape[0], dtype=jnp.int32)
    order = jnp.sum(jnp.where(assign[None, :] == slots[:, None], slots[None, :], 0), axis=1)
    edges = ctx_dev * jnp.arange(ctx_count + 1, dtype=jnp.int32)
    below = jnp.sum((kept[:, :, None, :] < edges[:, None]).astype(jnp.int32), axis=3)
    counts = below[:, :, 1:] - below[:, :, :-1]
    counts = jnp.transpose(counts.reshape(groups, 2, heads, ctx_count), (1, 0, 2, 3))
    offsets = jnp.arange(capacity, dtype=jnp.int32)
    bias = jnp.where(offsets < counts[..., None], 0.0, neg_large).astype(jnp.float32)
    bias = bias.reshape(2, groups, heads, ctx_count * capacity)
    new_sides = jnp.transpose(new_kv[0], (1, 0, 2)).reshape(2, heads, rows, width)
    places = places_of(
        kept.reshape(groups * kv_here, kept.shape[2]), ctx_id * ctx_dev, capacity
    )
    flat_cache = cache.reshape(groups * kv_here, ctx_dev, width)
    head_out = relayout_attend(flat_cache, places, order, groups, queries[0], new_sides, bias)
    return gather_project(head_out, out_weight, assign)


def solution(mesh):
    placed = (
        P("dp", "tensor", "ctx", None),
        P("dp", "tensor", None),
        P(),
        P("ctx", "dp", "tensor"),
        P("ctx", "dp", "tensor", None),
        P("tensor", "ctx"),
    )
    return jax.shard_map(
        local, mesh=mesh, in_specs=placed, out_specs=P("tensor", "dp", "ctx"), check_vma=False
    )
```

```python
import functools
import math

import jax
import jax.numpy as jnp
from jax import lax
from jax.experimental import pallas as pl
from jax.experimental.pallas import tpu as pltpu
from jax.sharding import PartitionSpec as P

neg_large = -1e30
MESH = pl.DeviceIdType.MESH


def swapped(array, axis, distance):
    return lax.ppermute(array, axis, [(i, i ^ 1 << distance) for i in range(lax.axis_size(axis))])


def slot_prompt(assign, slot_id):
    matches = (assign == slot_id).astype(jnp.int32)
    return jnp.sum(matches * jnp.arange(assign.shape[0], dtype=jnp.int32))


def block_rows_of(flat_cache, kept_lists, block_start, first_rank, row_count, stride, capacity):
    offsets = jnp.arange(capacity, dtype=jnp.int32)
    rank_ids = jnp.clip(first_rank[:, None] + stride * offsets[None, :], 0, kept_lists.shape[1] - 1)
    places = jnp.take_along_axis(kept_lists, rank_ids, axis=1) - block_start
    is_valid = offsets[None, :] < row_count[:, None]
    spots = jnp.arange(flat_cache.shape[1], dtype=jnp.int32)
    chooser = ((places[:, :, None] == spots[None, None, :]) & is_valid[:, :, None]).astype(
        flat_cache.dtype
    )
    picked = jnp.einsum("gcq,gqw->gcw", chooser, flat_cache, preferred_element_type=jnp.float32)
    return picked.astype(flat_cache.dtype)


def padded_layout(rows, marks):
    senders, kv_here, capacity, row_width = rows.shape
    flat_rows = jnp.transpose(rows, (1, 0, 2, 3)).reshape(kv_here, senders * capacity, row_width)
    flat_marks = jnp.transpose(marks, (1, 0, 2)).reshape(kv_here, senders * capacity)
    return (flat_rows, flat_marks)


def attend_rows(query, row_start, kept_rows, kept_marks, new_rows, new_start):
    head_dim = kept_rows.shape[2] // 2
    score_scale = head_dim ** (-0.5)
    kept_scores = (
        jnp.einsum(
            "rkgd,knd->rkgn", query, kept_rows[:, :, :head_dim], preferred_element_type=jnp.float32
        )
        * score_scale
    )
    kept_scores = jnp.where((kept_marks > 0.5)[None, :, None, :], kept_scores, neg_large)
    new_scores = (
        jnp.einsum(
            "rkgd,nkd->rkgn", query, new_rows[:, :, :head_dim], preferred_element_type=jnp.float32
        )
        * score_scale
    )
    row_ids = row_start + jnp.arange(query.shape[0], dtype=jnp.int32)
    key_ids = new_start + jnp.arange(new_rows.shape[0], dtype=jnp.int32)
    visible = (key_ids[None, :] <= row_ids[:, None])[:, None, None, :]
    new_scores = jnp.where(visible, new_scores, neg_large)
    row_top = jnp.maximum(jnp.max(kept_scores, axis=3), jnp.max(new_scores, axis=3))
    kept_weights = jnp.exp(kept_scores - row_top[..., None])
    new_weights = jnp.exp(new_scores - row_top[..., None])
    weight_sum = jnp.sum(kept_weights, axis=3) + jnp.sum(new_weights, axis=3)
    weighted = jnp.einsum(
        "rkgn,knd->rkgd",
        kept_weights.astype(jnp.bfloat16),
        kept_rows[:, :, head_dim:],
        preferred_element_type=jnp.float32,
    )
    weighted = weighted + jnp.einsum(
        "rkgn,nkd->rkgd",
        new_weights.astype(jnp.bfloat16),
        new_rows[:, :, head_dim:],
        preferred_element_type=jnp.float32,
    )
    return (row_top, weight_sum, weighted)


def attend(query, row_start, kept_rows, kept_marks, new_rows, new_start):
    half_rows = query.shape[0] // 2
    first = attend_rows(query[:half_rows], row_start, kept_rows, kept_marks, new_rows, new_start)
    second = attend_rows(
        query[half_rows:], row_start + half_rows, kept_rows, kept_marks, new_rows, new_start
    )
    return tuple((jnp.concatenate([first[index], second[index]], axis=0) for index in range(3)))


def local_by_rows(cache, kept, assign, queries, new_kv, out_weight):
    ctx_count = lax.axis_size("ctx")
    ctx_id = lax.axis_index("ctx")
    dp_id = lax.axis_index("dp")
    groups, kv_here, ctx_dev, row_width = cache.shape
    head_dim = row_width // 2
    keep_total = kept.shape[2]
    flat_cache = cache.reshape(groups * kv_here, ctx_dev, row_width)
    kept_lists = kept.reshape(groups * kv_here, keep_total)
    block_start = ctx_id * ctx_dev
    rank_low = jnp.sum((kept_lists < block_start).astype(jnp.int32), axis=1)
    rank_high = jnp.sum((kept_lists < block_start + ctx_dev).astype(jnp.int32), axis=1)
    slot_ids = lax.dynamic_slice_in_dim(assign, dp_id * groups, groups)
    prompt = slot_prompt(assign, ctx_id)
    capacity = ctx_dev // 2
    row_count = rank_high - rank_low
    picked = block_rows_of(flat_cache, kept_lists, block_start, rank_low, row_count, 1, capacity)
    picked = picked.reshape(groups, kv_here, capacity, row_width)
    buffer = (
        jnp.zeros((ctx_count, kv_here, capacity, row_width), cache.dtype).at[slot_ids].set(picked)
    )
    counts = (
        jnp.zeros((ctx_count, kv_here), jnp.int32)
        .at[slot_ids]
        .set(row_count.reshape(groups, kv_here))
    )
    received, got_counts = (
        lax.all_to_all(buffer, "ctx", split_axis=0, concat_axis=0, tiled=True),
        lax.all_to_all(counts, "ctx", split_axis=0, concat_axis=0, tiled=True),
    )
    halves = received.reshape(ctx_count, kv_here, capacity // 2, 2, row_width)
    offsets = jnp.arange(capacity // 2, dtype=jnp.int32)
    even_marks = (2 * offsets[None, None, :] < got_counts[:, :, None]).astype(cache.dtype)
    odd_marks = (2 * offsets[None, None, :] + 1 < got_counts[:, :, None]).astype(cache.dtype)
    own_rows = jnp.where(dp_id == 0, halves[:, :, :, 0], halves[:, :, :, 1])
    own_marks = jnp.where(dp_id == 0, even_marks, odd_marks)
    their_rows = jnp.where(dp_id == 0, halves[:, :, :, 1], halves[:, :, :, 0])
    their_marks = jnp.where(dp_id == 0, odd_marks, even_marks)
    own_flat, own_flat_marks = padded_layout(own_rows, own_marks)
    their_flat, their_flat_marks = padded_layout(their_rows, their_marks)
    from_partner, partner_marks = swapped((their_flat, their_flat_marks), "dp", 0)
    owner_here = prompt // groups == dp_id
    kept_half = jnp.where(owner_here, own_flat, from_partner)
    kept_marks = jnp.where(owner_here, own_flat_marks, partner_marks)
    rows_here = queries.shape[1]
    per_group = queries.shape[2] // (kv_here * head_dim)
    own_query = queries[0].reshape(rows_here, kv_here, per_group, head_dim)
    own_new = new_kv[0]
    own_start = dp_id * rows_here
    other_kept, other_marks, other_new = swapped((kept_half, kept_marks, own_new), "dp", 0)
    all_kept = jnp.concatenate([kept_half, other_kept], axis=1)
    all_marks = jnp.concatenate([kept_marks, other_marks], axis=1)
    all_new = jnp.where(
        dp_id == 0,
        jnp.concatenate([own_new, other_new], axis=0),
        jnp.concatenate([other_new, own_new], axis=0),
    )
    row_top, weight_sum, weighted = attend(own_query, own_start, all_kept, all_marks, all_new, 0)
    head_out = (
        (weighted / weight_sum[..., None])
        .reshape(rows_here, kv_here * per_group * head_dim)
        .astype(jnp.bfloat16)
    )
    partials = jnp.dot(
        lax.all_gather(head_out, "ctx", axis=0, tiled=True),
        out_weight,
        preferred_element_type=jnp.float32,
    )
    partials = partials.reshape(ctx_count, rows_here, partials.shape[1])[assign]
    return lax.psum_scatter(
        partials.astype(jnp.bfloat16), "tensor", scatter_dimension=0, tiled=True
    )


def places_kernel(start_ref, kept_ref, out_ref):
    start = start_ref[0]
    groups, kv_here, total = kept_ref.shape
    capacity = out_ref.shape[2]
    for i in range(groups * kv_here):
        g, h = i // kv_here, i % kv_here
        kept = kept_ref[g, h : h + 1]
        first = jnp.sum((kept < start).astype(jnp.int32))
        wide = jnp.broadcast_to(kept, (8, total))
        rolled = pltpu.roll(wide, lax.rem(total - first, total), 1)
        out_ref[i] = rolled[:1, :capacity] - start


def places_of(kept, block_start, capacity):
    return pl.pallas_call(
        places_kernel,
        out_shape=jax.ShapeDtypeStruct((kept.shape[0] * kept.shape[1], 1, capacity), jnp.int32),
        in_specs=[
            pl.BlockSpec(memory_space=pltpu.SMEM),
            pl.BlockSpec(memory_space=pltpu.VMEM),
        ],
        out_specs=pl.BlockSpec(memory_space=pltpu.VMEM),
    )(block_start.reshape(1), kept)


def relayout_kernel(
    order_ref, places_ref, cache_hbm, query_hbm, new_hbm, bias_hbm, head_out_ref,
    out_ref, query, new_rows, bias, cache, stage, outgoing,
    load_sem, y_send, y_recv, ctx_send, ctx_recv, side_send, side_recv, side_own, *pool
):
    c = lax.axis_index("ctx")
    d = lax.axis_index("dp")
    groups = stage.shape[1]
    slots = out_ref.shape[0]
    kv_here = cache_hbm.shape[0] // groups
    heads = kv_here // 2
    capacity, width = places_ref.shape[2], cache.shape[2]
    piece = stage.shape[2]
    pieces = capacity // piece

    def load(i):
        return pltpu.make_async_copy(cache_hbm.at[i], cache.at[i], load_sem.at[i])

    for j in range(heads):
        for side in (1 - d, d):
            for g in range(groups):
                load(g * kv_here + side * heads + j).start()

    barrier = pltpu.get_barrier_semaphore()
    pl.semaphore_signal(barrier, inc=1, device_id={"dp": 1 - d}, device_id_type=MESH)
    for k in range(1, slots):
        pl.semaphore_signal(
            barrier, inc=1, device_id={"ctx": lax.rem(c + k, slots)}, device_id_type=MESH
        )
    pl.semaphore_wait(barrier, slots)

    rows, columns = query_hbm.shape[0], query.shape[1]

    def side_parts(side, place):
        across = pl.ds(pl.multiple_of(side * columns, columns), columns)
        down = pl.ds(pl.multiple_of(place * rows, rows), rows)
        return (
            (query_hbm.at[:, across], query.at[down]),
            (new_hbm.at[side], new_rows.at[:, down]),
            (bias_hbm.at[side], bias.at[pl.ds(place * groups, groups)]),
        )

    def side_sends(place):
        return [
            pltpu.make_async_remote_copy(
                src_ref=source, dst_ref=target, send_sem=side_send.at[i], recv_sem=side_recv.at[i],
                device_id={"dp": 1 - d}, device_id_type=MESH,
            )
            for i, (source, target) in enumerate(side_parts(1 - d, place))
        ]

    own_parts = [
        pltpu.make_async_copy(source, target, side_own.at[i])
        for i, (source, target) in enumerate(side_parts(d, d))
    ]
    for part in own_parts:
        part.start()

    spot_ids = lax.broadcasted_iota(jnp.int32, (cache.shape[1], capacity), 0)

    def pick(i):
        load(i).wait()
        chooser = (spot_ids == places_ref[i]).astype(jnp.float32).astype(jnp.bfloat16)
        return lax.dot_general(
            chooser, cache[i], (((0,), (0,)), ((), ())), preferred_element_type=jnp.float32
        ).astype(cache.dtype)

    def y_copy(q, g, sender):
        return pltpu.make_async_remote_copy(
            src_ref=stage.at[q, g], dst_ref=pool[q].at[sender * groups + g], send_sem=y_send.at[q, g],
            recv_sem=y_recv.at[q, g], device_id={"dp": 1 - d}, device_id_type=MESH,
        )

    def ctx_copy(q, k):
        span = pl.ds((q % pieces) * piece, piece)
        return pltpu.make_async_remote_copy(
            src_ref=outgoing.at[q, k - 1], dst_ref=out_ref.at[c, q // pieces, span],
            send_sem=ctx_send.at[q, k - 1], recv_sem=ctx_recv.at[q, k - 1],
            device_id={"ctx": lax.rem(c + k, slots)}, device_id_type=MESH,
        )

    def pick_theirs(j):
        def step(g, carry):
            picked = pick(g * kv_here + (1 - d) * heads + j)
            for half in range(pieces):
                stage[j * pieces + half, g] = picked[half * piece : (half + 1) * piece]
            y_copy(j * pieces, g, d).start()
            return carry

        lax.fori_loop(0, groups, step, 0)
        for half in range(1, pieces):
            for g in range(groups):
                y_copy(j * pieces + half, g, d).start()

    def pick_mine(j):
        def step(g, carry):
            picked = pick(g * kv_here + d * heads + j)
            for half in range(pieces):
                pool[j * pieces + half][d * groups + g] = picked[half * piece : (half + 1) * piece]
            return carry

        lax.fori_loop(0, groups, step, 0)

    def scatter(q):
        for g in range(groups):
            y_copy(q, g, 1 - d).wait_recv()
        for k in (4, 5, 3, 2, 6, 1, 7) if slots == 8 else range(1, slots):
            outgoing[q, k - 1] = pool[q][order_ref[lax.rem(c + k, slots)]]
            ctx_copy(q, k).start()
        start = (q % pieces) * piece
        out_ref[c, q // pieces, start : start + piece] = pool[q][order_ref[c]]

    pick_theirs(0)
    pick_mine(0)
    for j in range(heads):
        if j + 1 < heads:
            pick_theirs(j + 1)
        for half in range(pieces):
            scatter(j * pieces + half)
            if half == 0 and j + 1 < heads:
                pick_mine(j + 1)
            if half == 0 and j == 0:
                for part in side_sends(d):
                    part.start()

    def finish(q):
        for k in range(1, slots):
            sender = lax.rem(c + slots - k, slots)
            start = (q % pieces) * piece
            pltpu.make_async_remote_copy(
                src_ref=outgoing.at[q, k - 1],
                dst_ref=out_ref.at[sender, q // pieces, pl.ds(start, piece)],
                send_sem=ctx_send.at[q, k - 1], recv_sem=ctx_recv.at[q, k - 1],
                device_id={"ctx": lax.rem(c + k, slots)}, device_id_type=MESH,
            ).wait()
        for g in range(groups):
            y_copy(q, g, d).wait_send()

    hd = width // 2
    tiles = columns // heads // (2 * hd)
    for h in range(heads):
        for half in range(pieces):
            finish(h * pieces + half)
        if h == 0:
            for part in own_parts:
                part.wait()
            for part in side_sends(1 - d):
                part.wait_recv()

        def tile_step(n, carry):
            low = pl.multiple_of((h * tiles + n) * 2 * hd, 2 * hd)
            first, second = attend_tile(
                query[:, pl.ds(low, hd)], query[:, pl.ds(low + hd, hd)],
                out_ref[:, h], bias[order_ref[c], h : h + 1], new_rows[h],
            )
            head_out_ref[:, pl.ds(low, hd)] = first
            head_out_ref[:, pl.ds(low + hd, hd)] = second
            return carry

        lax.fori_loop(0, tiles, tile_step, 0)
    for part in side_sends(d):
        part.wait_send()


def relayout_attend(flat_cache, places, order, groups, queries, new_sides, bias_sides):
    lists, spots, width = flat_cache.shape
    capacity = places.shape[2]
    slots = order.shape[0]
    heads = lists // groups // 2
    pieces = 2
    piece = capacity // pieces
    kind = flat_cache.dtype
    rows, columns = queries.shape[0], queries.shape[1] // 2
    dma = pltpu.SemaphoreType.DMA
    return pl.pallas_call(
        relayout_kernel,
        out_shape=jax.ShapeDtypeStruct((2 * rows, columns), kind),
        in_specs=[
            pl.BlockSpec(memory_space=pltpu.SMEM),
            pl.BlockSpec(memory_space=pltpu.VMEM),
            pl.BlockSpec(memory_space=pl.ANY),
            pl.BlockSpec(memory_space=pl.ANY),
            pl.BlockSpec(memory_space=pltpu.VMEM),
            pl.BlockSpec(memory_space=pltpu.VMEM),
        ],
        out_specs=pl.BlockSpec(memory_space=pltpu.VMEM),
        scratch_shapes=[
            pltpu.VMEM((slots, heads, capacity, width), kind),
            pltpu.VMEM((2 * rows, columns), kind),
            pltpu.VMEM((heads, 2 * rows, width), kind),
            pltpu.VMEM((2 * groups,) + bias_sides.shape[2:], jnp.float32),
            pltpu.VMEM((lists, spots, width), kind),
            pltpu.VMEM((heads * pieces, groups, piece, width), kind),
            pltpu.VMEM((heads * pieces, slots - 1, piece, width), kind),
            dma((lists,)),
            dma((heads * pieces, groups)),
            dma((heads * pieces, groups)),
            dma((heads * pieces, slots - 1)),
            dma((heads * pieces, slots - 1)),
            dma((3,)),
            dma((3,)),
            dma((3,)),
        ]
        + [pltpu.VMEM((2 * groups, piece, width), kind)] * (heads * pieces),
        cost_estimate=pl.CostEstimate(flops=int(3e10), bytes_accessed=int(1.5e8), transcendentals=0),
        compiler_params=pltpu.CompilerParams(
            collective_id=0, has_side_effects=True, vmem_limit_bytes=60 * 1024 * 1024
        ),
    )(order, places, flat_cache, queries, new_sides, bias_sides)


def attend_tile(first_query, second_query, received, bias, new_rows):
    blocks, capacity, width = received.shape
    rows, hd = first_query.shape
    q = jnp.concatenate([first_query, second_query], axis=0)
    keys = received[:, :, :hd].reshape(blocks * capacity, hd)
    values = received[:, :, hd:].reshape(blocks * capacity, hd)
    new_keys = new_rows[:, :hd]
    new_values = new_rows[:, hd:]
    scale = hd**-0.5 * math.log2(math.e)
    dims = (((1,), (1,)), ((), ()))
    kept_scores = lax.dot_general(q, keys, dims, preferred_element_type=jnp.float32) * scale
    kept_scores = kept_scores + bias
    new_scores = lax.dot_general(q, new_keys, dims, preferred_element_type=jnp.float32) * scale
    row_ids = lax.rem(lax.broadcasted_iota(jnp.int32, new_scores.shape, 0), rows)
    key_ids = lax.broadcasted_iota(jnp.int32, new_scores.shape, 1)
    new_scores = jnp.where(key_ids <= row_ids, new_scores, neg_large)
    top = jnp.maximum(
        jnp.max(kept_scores, axis=1, keepdims=True), jnp.max(new_scores, axis=1, keepdims=True)
    )
    kept_weights = jnp.exp2(kept_scores - top)
    new_weights = jnp.exp2(new_scores - top)
    total = jnp.sum(kept_weights, axis=1, keepdims=True) + jnp.sum(new_weights, axis=1, keepdims=True)
    weighted = jnp.dot(
        kept_weights.astype(jnp.bfloat16), values, preferred_element_type=jnp.float32
    ) + jnp.dot(new_weights.astype(jnp.bfloat16), new_values, preferred_element_type=jnp.float32)
    result = (weighted / total).astype(first_query.dtype)
    return result[:rows], result[rows:]


def gather_project_kernel(
    assign_ref, heads_ref, weight_hbm, out_ref,
    gat, weight, part, send_buf, recv_buf,
    send, recv, y_send, core_send, core_recv, weight_sem,
):
    c = lax.axis_index("ctx")
    t = lax.axis_index("tensor")
    d = lax.axis_index("dp")
    z, x = c // 2, c % 2
    zs = gat.shape[1] // 2
    rows = gat.shape[2]
    tile = part.shape[3]
    partner_x = z * 2 + 1 - x
    kept = out_ref.shape[0]

    load_weight = pltpu.make_async_copy(weight_hbm, weight, weight_sem)
    load_weight.start()
    barrier = pltpu.get_barrier_semaphore()
    for target in ({"ctx": partner_x}, {"dp": 1 - d}, {"tensor": 1 - t}):
        pl.semaphore_signal(barrier, inc=1, device_id=target, device_id_type=MESH)

    @pl.when(z > 0)
    def _():
        pl.semaphore_signal(barrier, inc=1, device_id={"ctx": c - 2}, device_id_type=MESH)

    @pl.when(z < zs - 1)
    def _():
        pl.semaphore_signal(barrier, inc=1, device_id={"ctx": c + 2}, device_id_type=MESH)

    pl.semaphore_wait(barrier, 3 + (z > 0).astype(jnp.int32) + (z < zs - 1).astype(jnp.int32))

    cut = rows // 4
    spans = ((d, 0, cut), (d, cut, rows), (1 - d, 0, rows // 2), (1 - d, rows // 2, rows))
    x_first = (0,)
    z_first = (1, 2, 3)

    def copy(piece, slot, channel):
        col, low, high = spans[piece]
        ref = gat.at[col, slot, pl.ds(low, high - low)]
        target = (c + 2, c - 2, partner_x)[channel]
        return pltpu.make_async_remote_copy(
            src_ref=ref, dst_ref=ref, send_sem=send.at[piece, slot, channel],
            recv_sem=recv.at[piece, slot], device_id={"ctx": target}, device_id_type=MESH,
        )

    def up(piece, slot):
        @pl.when(z < zs - 1)
        def _():
            copy(piece, slot, 0).start()

    def down(piece, slot):
        @pl.when(z > 0)
        def _():
            copy(piece, slot, 1).start()

    def arrived(piece, slot):
        copy(piece, slot, 2).wait_recv()

    def y_copy(piece):
        _, low, high = spans[piece]
        return pltpu.make_async_remote_copy(
            src_ref=heads_ref.at[pl.ds(pl.multiple_of((1 - d) * rows + low, 16), high - low)],
            dst_ref=gat.at[d, c, pl.ds(low, high - low)],
            send_sem=y_send.at[piece - 2], recv_sem=recv.at[piece, c],
            device_id={"dp": 1 - d}, device_id_type=MESH,
        )

    y_copy(2).start()
    y_copy(3).start()
    gat[d, c] = heads_ref[pl.ds(pl.multiple_of(d * rows, rows), rows)]
    copy(0, c, 2).start()
    up(1, c)
    down(1, c)
    copy(1, c, 2).start()
    up(0, c)
    down(0, c)
    for piece in (2, 3):
        arrived(piece, c)
        up(piece, c)
        down(piece, c)
        copy(piece, c, 2).start()
    arrived(0, partner_x)
    up(0, partner_x)
    down(0, partner_x)
    slots = gat.shape[1]
    depth = gat.shape[3]
    tiles = part.shape[0]
    near = z // 2 * (slots // 2)
    far = slots // 2 - near

    def multiply(n, first):
        span = pl.ds(pl.multiple_of(n * tile, tile), tile)
        some = pl.ds(first, slots // 2)
        flat = (slots // 2 * rows, depth)
        product = jnp.dot(
            gat[0, some].reshape(flat), weight[:depth, span], preferred_element_type=jnp.float32
        ) + jnp.dot(
            gat[1, some].reshape(flat), weight[depth:, span], preferred_element_type=jnp.float32
        )
        part[n, some] = product.reshape(slots // 2, rows, tile)

    for k in range(1, zs):
        if k == zs - 1:
            for piece in z_first:
                for zo in range(2):
                    arrived(piece, near + zo * 2 + 1 - x)
            load_weight.wait()
        for index, piece in enumerate((1, 0, 2, 3)):
            if k == zs - 1:
                for n in range(index * tiles // 4, (index + 1) * tiles // 4):
                    multiply(n, near)
            for base in (c, partner_x) if piece in x_first else (c,):
                @pl.when(z >= k)
                def _():
                    arrived(piece, base - 2 * k)
                    up(piece, base - 2 * k)
                    if piece in z_first:
                        copy(piece, base - 2 * k, 2).start()

                @pl.when(z + k < zs)
                def _():
                    arrived(piece, base + 2 * k)
                    down(piece, base + 2 * k)
                    if piece in z_first:
                        copy(piece, base + 2 * k, 2).start()

    for piece in z_first:
        for zo in range(2):
            arrived(piece, far + zo * 2 + 1 - x)

    def exchange(n):
        return pltpu.make_async_remote_copy(
            src_ref=send_buf.at[n], dst_ref=recv_buf.at[n], send_sem=core_send.at[n],
            recv_sem=core_recv.at[n], device_id={"tensor": 1 - t}, device_id_type=MESH,
        )

    def tile_step(n, carry):
        multiply(n, far)
        for j in range(kept):
            send_buf[n, j] = part[n, assign_ref[(1 - t) * kept + j]].astype(send_buf.dtype)
        exchange(n).start()
        return carry

    lax.fori_loop(0, tiles, tile_step, 0)
    for n in range(tiles):
        exchange(n).wait_recv()
        for j in range(kept):
            total = part[n, assign_ref[t * kept + j]] + recv_buf[n, j].astype(jnp.float32)
            out_ref[j, :, n * tile : (n + 1) * tile] = total.astype(out_ref.dtype)

    y_copy(2).wait_send()
    y_copy(3).wait_send()
    for n in range(tiles):
        exchange(n).wait_send()
    for piece in x_first + z_first:
        copy(piece, c, 2).wait_send()
        for base in (c, partner_x) if piece in x_first else (c,):
            @pl.when(z < zs - 1)
            def _():
                copy(piece, base, 0).wait_send()

            @pl.when(z > 0)
            def _():
                copy(piece, base, 1).wait_send()

            for k in range(1, zs):
                @pl.when(z >= k)
                def _():
                    if piece in z_first:
                        copy(piece, base - 2 * k, 2).wait_send()

                    @pl.when(z < zs - 1)
                    def _():
                        copy(piece, base - 2 * k, 0).wait_send()

                @pl.when(z + k < zs)
                def _():
                    if piece in z_first:
                        copy(piece, base + 2 * k, 2).wait_send()

                    @pl.when(z > 0)
                    def _():
                        copy(piece, base + 2 * k, 1).wait_send()


def gather_project(head_out, out_weight, assign):
    slots = assign.shape[0]
    rows, half_depth = head_out.shape[0] // 2, head_out.shape[1]
    depth, columns = out_weight.shape
    kept = slots // 2
    tile = 256
    tiles = columns // tile
    kind = head_out.dtype
    dma = pltpu.SemaphoreType.DMA
    return pl.pallas_call(
        gather_project_kernel,
        out_shape=jax.ShapeDtypeStruct((kept, rows, columns), kind),
        in_specs=[
            pl.BlockSpec(memory_space=pltpu.SMEM),
            pl.BlockSpec(memory_space=pltpu.VMEM),
            pl.BlockSpec(memory_space=pl.ANY),
        ],
        out_specs=pl.BlockSpec(memory_space=pltpu.VMEM),
        scratch_shapes=[
            pltpu.VMEM((2, slots, rows, half_depth), kind),
            pltpu.VMEM((depth, columns), kind),
            pltpu.VMEM((tiles, slots, rows, tile), jnp.float32),
            pltpu.VMEM((tiles, kept, rows, tile), kind),
            pltpu.VMEM((tiles, kept, rows, tile), kind),
            dma((4, slots, 3)),
            dma((4, slots)),
            dma((2,)),
            dma((tiles,)),
            dma((tiles,)),
            dma,
        ],
        compiler_params=pltpu.CompilerParams(
            collective_id=1, has_side_effects=True, vmem_limit_bytes=60 * 1024 * 1024
        ),
    )(assign, head_out, out_weight)


def local(cache, kept, assign, queries, new_kv, out_weight):
    groups, kv_here, ctx_dev, width = cache.shape
    ctx_count = lax.axis_size("ctx")
    if kv_here % 2 or ctx_count != 8 or lax.axis_size("tensor") != 2:
        return local_by_rows(cache, kept, assign, queries, new_kv, out_weight)
    ctx_id = lax.axis_index("ctx")
    capacity = ctx_dev // 2
    heads = kv_here // 2
    rows = queries.shape[1]
    slots = jnp.arange(assign.shape[0], dtype=jnp.int32)
    order = jnp.sum(jnp.where(assign[None, :] == slots[:, None], slots[None, :], 0), axis=1)
    edges = ctx_dev * jnp.arange(ctx_count + 1, dtype=jnp.int32)
    below = jnp.sum((kept[:, :, None, :] < edges[:, None]).astype(jnp.int32), axis=3)
    counts = below[:, :, 1:] - below[:, :, :-1]
    counts = jnp.transpose(counts.reshape(groups, 2, heads, ctx_count), (1, 0, 2, 3))
    offsets = jnp.arange(capacity, dtype=jnp.int32)
    bias = jnp.where(offsets < counts[..., None], 0.0, neg_large).astype(jnp.float32)
    bias = bias.reshape(2, groups, heads, ctx_count * capacity)
    new_sides = jnp.transpose(new_kv[0], (1, 0, 2)).reshape(2, heads, rows, width)
    places = places_of(kept, ctx_id * ctx_dev, capacity)
    flat_cache = cache.reshape(groups * kv_here, ctx_dev, width)
    head_out = relayout_attend(flat_cache, places, order, groups, queries[0], new_sides, bias)
    return gather_project(head_out, out_weight, assign)


def solution(mesh):
    placed = (
        P("dp", "tensor", "ctx", None),
        P("dp", "tensor", None),
        P(),
        P("ctx", "dp", "tensor"),
        P("ctx", "dp", "tensor", None),
        P("tensor", "ctx"),
    )
    return jax.shard_map(
        local, mesh=mesh, in_specs=placed, out_specs=P("tensor", "dp", "ctx"), check_vma=False
    )
```

```python
import functools
import math

import jax
import jax.numpy as jnp
from jax import lax
from jax.experimental import pallas as pl
from jax.experimental.pallas import tpu as pltpu
from jax.sharding import PartitionSpec as P

neg_large = -1e30
MESH = pl.DeviceIdType.MESH


def swapped(array, axis, distance):
    return lax.ppermute(array, axis, [(i, i ^ 1 << distance) for i in range(lax.axis_size(axis))])


def slot_prompt(assign, slot_id):
    matches = (assign == slot_id).astype(jnp.int32)
    return jnp.sum(matches * jnp.arange(assign.shape[0], dtype=jnp.int32))


def block_rows_of(flat_cache, kept_lists, block_start, first_rank, row_count, stride, capacity):
    offsets = jnp.arange(capacity, dtype=jnp.int32)
    rank_ids = jnp.clip(first_rank[:, None] + stride * offsets[None, :], 0, kept_lists.shape[1] - 1)
    places = jnp.take_along_axis(kept_lists, rank_ids, axis=1) - block_start
    is_valid = offsets[None, :] < row_count[:, None]
    spots = jnp.arange(flat_cache.shape[1], dtype=jnp.int32)
    chooser = ((places[:, :, None] == spots[None, None, :]) & is_valid[:, :, None]).astype(
        flat_cache.dtype
    )
    picked = jnp.einsum("gcq,gqw->gcw", chooser, flat_cache, preferred_element_type=jnp.float32)
    return picked.astype(flat_cache.dtype)


def padded_layout(rows, marks):
    senders, kv_here, capacity, row_width = rows.shape
    flat_rows = jnp.transpose(rows, (1, 0, 2, 3)).reshape(kv_here, senders * capacity, row_width)
    flat_marks = jnp.transpose(marks, (1, 0, 2)).reshape(kv_here, senders * capacity)
    return (flat_rows, flat_marks)


def attend_rows(query, row_start, kept_rows, kept_marks, new_rows, new_start):
    head_dim = kept_rows.shape[2] // 2
    score_scale = head_dim ** (-0.5)
    kept_scores = (
        jnp.einsum(
            "rkgd,knd->rkgn", query, kept_rows[:, :, :head_dim], preferred_element_type=jnp.float32
        )
        * score_scale
    )
    kept_scores = jnp.where((kept_marks > 0.5)[None, :, None, :], kept_scores, neg_large)
    new_scores = (
        jnp.einsum(
            "rkgd,nkd->rkgn", query, new_rows[:, :, :head_dim], preferred_element_type=jnp.float32
        )
        * score_scale
    )
    row_ids = row_start + jnp.arange(query.shape[0], dtype=jnp.int32)
    key_ids = new_start + jnp.arange(new_rows.shape[0], dtype=jnp.int32)
    visible = (key_ids[None, :] <= row_ids[:, None])[:, None, None, :]
    new_scores = jnp.where(visible, new_scores, neg_large)
    row_top = jnp.maximum(jnp.max(kept_scores, axis=3), jnp.max(new_scores, axis=3))
    kept_weights = jnp.exp(kept_scores - row_top[..., None])
    new_weights = jnp.exp(new_scores - row_top[..., None])
    weight_sum = jnp.sum(kept_weights, axis=3) + jnp.sum(new_weights, axis=3)
    weighted = jnp.einsum(
        "rkgn,knd->rkgd",
        kept_weights.astype(jnp.bfloat16),
        kept_rows[:, :, head_dim:],
        preferred_element_type=jnp.float32,
    )
    weighted = weighted + jnp.einsum(
        "rkgn,nkd->rkgd",
        new_weights.astype(jnp.bfloat16),
        new_rows[:, :, head_dim:],
        preferred_element_type=jnp.float32,
    )
    return (row_top, weight_sum, weighted)


def attend(query, row_start, kept_rows, kept_marks, new_rows, new_start):
    half_rows = query.shape[0] // 2
    first = attend_rows(query[:half_rows], row_start, kept_rows, kept_marks, new_rows, new_start)
    second = attend_rows(
        query[half_rows:], row_start + half_rows, kept_rows, kept_marks, new_rows, new_start
    )
    return tuple((jnp.concatenate([first[index], second[index]], axis=0) for index in range(3)))


def local_by_rows(cache, kept, assign, queries, new_kv, out_weight):
    ctx_count = lax.axis_size("ctx")
    ctx_id = lax.axis_index("ctx")
    dp_id = lax.axis_index("dp")
    groups, kv_here, ctx_dev, row_width = cache.shape
    head_dim = row_width // 2
    keep_total = kept.shape[2]
    flat_cache = cache.reshape(groups * kv_here, ctx_dev, row_width)
    kept_lists = kept.reshape(groups * kv_here, keep_total)
    block_start = ctx_id * ctx_dev
    rank_low = jnp.sum((kept_lists < block_start).astype(jnp.int32), axis=1)
    rank_high = jnp.sum((kept_lists < block_start + ctx_dev).astype(jnp.int32), axis=1)
    slot_ids = lax.dynamic_slice_in_dim(assign, dp_id * groups, groups)
    prompt = slot_prompt(assign, ctx_id)
    capacity = ctx_dev // 2
    row_count = rank_high - rank_low
    picked = block_rows_of(flat_cache, kept_lists, block_start, rank_low, row_count, 1, capacity)
    picked = picked.reshape(groups, kv_here, capacity, row_width)
    buffer = (
        jnp.zeros((ctx_count, kv_here, capacity, row_width), cache.dtype).at[slot_ids].set(picked)
    )
    counts = (
        jnp.zeros((ctx_count, kv_here), jnp.int32)
        .at[slot_ids]
        .set(row_count.reshape(groups, kv_here))
    )
    received, got_counts = (
        lax.all_to_all(buffer, "ctx", split_axis=0, concat_axis=0, tiled=True),
        lax.all_to_all(counts, "ctx", split_axis=0, concat_axis=0, tiled=True),
    )
    halves = received.reshape(ctx_count, kv_here, capacity // 2, 2, row_width)
    offsets = jnp.arange(capacity // 2, dtype=jnp.int32)
    even_marks = (2 * offsets[None, None, :] < got_counts[:, :, None]).astype(cache.dtype)
    odd_marks = (2 * offsets[None, None, :] + 1 < got_counts[:, :, None]).astype(cache.dtype)
    own_rows = jnp.where(dp_id == 0, halves[:, :, :, 0], halves[:, :, :, 1])
    own_marks = jnp.where(dp_id == 0, even_marks, odd_marks)
    their_rows = jnp.where(dp_id == 0, halves[:, :, :, 1], halves[:, :, :, 0])
    their_marks = jnp.where(dp_id == 0, odd_marks, even_marks)
    own_flat, own_flat_marks = padded_layout(own_rows, own_marks)
    their_flat, their_flat_marks = padded_layout(their_rows, their_marks)
    from_partner, partner_marks = swapped((their_flat, their_flat_marks), "dp", 0)
    owner_here = prompt // groups == dp_id
    kept_half = jnp.where(owner_here, own_flat, from_partner)
    kept_marks = jnp.where(owner_here, own_flat_marks, partner_marks)
    rows_here = queries.shape[1]
    per_group = queries.shape[2] // (kv_here * head_dim)
    own_query = queries[0].reshape(rows_here, kv_here, per_group, head_dim)
    own_new = new_kv[0]
    own_start = dp_id * rows_here
    other_kept, other_marks, other_new = swapped((kept_half, kept_marks, own_new), "dp", 0)
    all_kept = jnp.concatenate([kept_half, other_kept], axis=1)
    all_marks = jnp.concatenate([kept_marks, other_marks], axis=1)
    all_new = jnp.where(
        dp_id == 0,
        jnp.concatenate([own_new, other_new], axis=0),
        jnp.concatenate([other_new, own_new], axis=0),
    )
    row_top, weight_sum, weighted = attend(own_query, own_start, all_kept, all_marks, all_new, 0)
    head_out = (
        (weighted / weight_sum[..., None])
        .reshape(rows_here, kv_here * per_group * head_dim)
        .astype(jnp.bfloat16)
    )
    partials = jnp.dot(
        lax.all_gather(head_out, "ctx", axis=0, tiled=True),
        out_weight,
        preferred_element_type=jnp.float32,
    )
    partials = partials.reshape(ctx_count, rows_here, partials.shape[1])[assign]
    return lax.psum_scatter(
        partials.astype(jnp.bfloat16), "tensor", scatter_dimension=0, tiled=True
    )


def places_kernel(start_ref, kept_ref, out_ref):
    start = start_ref[0]
    groups, kv_here, total = kept_ref.shape
    capacity = out_ref.shape[2]
    for i in range(groups * kv_here):
        g, h = i // kv_here, i % kv_here
        kept = kept_ref[g, h : h + 1]
        first = jnp.sum((kept < start).astype(jnp.int32))
        wide = jnp.broadcast_to(kept, (8, total))
        rolled = pltpu.roll(wide, lax.rem(total - first, total), 1)
        out_ref[i] = rolled[:1, :capacity] - start


def places_of(kept, block_start, capacity):
    return pl.pallas_call(
        places_kernel,
        out_shape=jax.ShapeDtypeStruct((kept.shape[0] * kept.shape[1], 1, capacity), jnp.int32),
        in_specs=[
            pl.BlockSpec(memory_space=pltpu.SMEM),
            pl.BlockSpec(memory_space=pltpu.VMEM),
        ],
        out_specs=pl.BlockSpec(memory_space=pltpu.VMEM),
    )(block_start.reshape(1), kept)


def relayout_kernel(
    order_ref, places_ref, cache_hbm, query_hbm, new_hbm, bias_hbm, head_out_ref,
    out_ref, query, new_rows, bias, cache, stage, outgoing,
    load_sem, y_send, y_recv, ctx_send, ctx_recv, side_send, side_recv, side_own, *pool
):
    c = lax.axis_index("ctx")
    d = lax.axis_index("dp")
    groups = stage.shape[1]
    slots = out_ref.shape[0]
    kv_here = cache_hbm.shape[0] // groups
    heads = kv_here // 2
    capacity, width = places_ref.shape[2], cache.shape[2]
    piece = stage.shape[2]
    pieces = capacity // piece

    def load(i):
        return pltpu.make_async_copy(cache_hbm.at[i], cache.at[i], load_sem.at[i])

    for j in range(heads):
        for side in (1 - d, d):
            for g in range(groups):
                load(g * kv_here + side * heads + j).start()

    barrier = pltpu.get_barrier_semaphore()
    pl.semaphore_signal(barrier, inc=1, device_id={"dp": 1 - d}, device_id_type=MESH)
    for k in range(1, slots):
        pl.semaphore_signal(
            barrier, inc=1, device_id={"ctx": lax.rem(c + k, slots)}, device_id_type=MESH
        )
    pl.semaphore_wait(barrier, slots)

    rows, columns = query_hbm.shape[0], query.shape[1]

    def side_parts(side, place):
        across = pl.ds(pl.multiple_of(side * columns, columns), columns)
        down = pl.ds(pl.multiple_of(place * rows, rows), rows)
        return (
            (query_hbm.at[:, across], query.at[down]),
            (new_hbm.at[side], new_rows.at[:, down]),
            (bias_hbm.at[side], bias.at[pl.ds(place * groups, groups)]),
        )

    def side_sends(place):
        return [
            pltpu.make_async_remote_copy(
                src_ref=source, dst_ref=target, send_sem=side_send.at[i], recv_sem=side_recv.at[i],
                device_id={"dp": 1 - d}, device_id_type=MESH,
            )
            for i, (source, target) in enumerate(side_parts(1 - d, place))
        ]

    own_parts = [
        pltpu.make_async_copy(source, target, side_own.at[i])
        for i, (source, target) in enumerate(side_parts(d, d))
    ]
    for part in own_parts:
        part.start()

    spot_ids = lax.broadcasted_iota(jnp.int32, (cache.shape[1], capacity), 0)

    def pick(i):
        load(i).wait()
        chooser = (spot_ids == places_ref[i]).astype(jnp.float32).astype(jnp.bfloat16)
        return lax.dot_general(
            chooser, cache[i], (((0,), (0,)), ((), ())), preferred_element_type=jnp.float32
        ).astype(cache.dtype)

    def y_copy(q, g, sender):
        return pltpu.make_async_remote_copy(
            src_ref=stage.at[q, g], dst_ref=pool[q].at[sender * groups + g], send_sem=y_send.at[q, g],
            recv_sem=y_recv.at[q, g], device_id={"dp": 1 - d}, device_id_type=MESH,
        )

    def ctx_copy(q, k):
        span = pl.ds((q % pieces) * piece, piece)
        return pltpu.make_async_remote_copy(
            src_ref=outgoing.at[q, k - 1], dst_ref=out_ref.at[c, q // pieces, span],
            send_sem=ctx_send.at[q, k - 1], recv_sem=ctx_recv.at[q, k - 1],
            device_id={"ctx": lax.rem(c + k, slots)}, device_id_type=MESH,
        )

    def pick_theirs(j):
        def step(g, carry):
            picked = pick(g * kv_here + (1 - d) * heads + j)
            for half in range(pieces):
                stage[j * pieces + half, g] = picked[half * piece : (half + 1) * piece]
            y_copy(j * pieces, g, d).start()
            return carry

        lax.fori_loop(0, groups, step, 0)
        for half in range(1, pieces):
            for g in range(groups):
                y_copy(j * pieces + half, g, d).start()

    def pick_mine(j):
        def step(g, carry):
            picked = pick(g * kv_here + d * heads + j)
            for half in range(pieces):
                pool[j * pieces + half][d * groups + g] = picked[half * piece : (half + 1) * piece]
            return carry

        lax.fori_loop(0, groups, step, 0)

    def scatter(q):
        for g in range(groups):
            y_copy(q, g, 1 - d).wait_recv()
        for k in (4, 5, 3, 2, 6, 1, 7) if slots == 8 else range(1, slots):
            outgoing[q, k - 1] = pool[q][order_ref[lax.rem(c + k, slots)]]
            ctx_copy(q, k).start()
        start = (q % pieces) * piece
        out_ref[c, q // pieces, start : start + piece] = pool[q][order_ref[c]]

    pick_theirs(0)
    pick_mine(0)
    for j in range(heads):
        if j + 1 < heads:
            pick_theirs(j + 1)
        for half in range(pieces):
            scatter(j * pieces + half)
            if half == 0 and j + 1 < heads:
                pick_mine(j + 1)
            if half == 0 and j == 0:
                for part in side_sends(d):
                    part.start()

    def finish(q):
        for k in range(1, slots):
            sender = lax.rem(c + slots - k, slots)
            start = (q % pieces) * piece
            pltpu.make_async_remote_copy(
                src_ref=outgoing.at[q, k - 1],
                dst_ref=out_ref.at[sender, q // pieces, pl.ds(start, piece)],
                send_sem=ctx_send.at[q, k - 1], recv_sem=ctx_recv.at[q, k - 1],
                device_id={"ctx": lax.rem(c + k, slots)}, device_id_type=MESH,
            ).wait()
        for g in range(groups):
            y_copy(q, g, d).wait_send()

    hd = width // 2
    tiles = columns // heads // (2 * hd)
    for h in range(heads):
        for half in range(pieces):
            finish(h * pieces + half)
        if h == 0:
            for part in own_parts:
                part.wait()
            for part in side_sends(1 - d):
                part.wait_recv()

        def tile_step(n, carry):
            low = pl.multiple_of((h * tiles + n) * 2 * hd, 2 * hd)
            first, second = attend_tile(
                query[:, pl.ds(low, hd)], query[:, pl.ds(low + hd, hd)],
                out_ref[:, h], bias[order_ref[c], h : h + 1], new_rows[h],
            )
            head_out_ref[:, pl.ds(low, hd)] = first
            head_out_ref[:, pl.ds(low + hd, hd)] = second
            return carry

        lax.fori_loop(0, tiles, tile_step, 0)
    for part in side_sends(d):
        part.wait_send()


def relayout_attend(flat_cache, places, order, groups, queries, new_sides, bias_sides):
    lists, spots, width = flat_cache.shape
    capacity = places.shape[2]
    slots = order.shape[0]
    heads = lists // groups // 2
    pieces = 2
    piece = capacity // pieces
    kind = flat_cache.dtype
    rows, columns = queries.shape[0], queries.shape[1] // 2
    dma = pltpu.SemaphoreType.DMA
    return pl.pallas_call(
        relayout_kernel,
        out_shape=jax.ShapeDtypeStruct((2 * rows, columns), kind),
        in_specs=[
            pl.BlockSpec(memory_space=pltpu.SMEM),
            pl.BlockSpec(memory_space=pltpu.VMEM),
            pl.BlockSpec(memory_space=pl.ANY),
            pl.BlockSpec(memory_space=pl.ANY),
            pl.BlockSpec(memory_space=pltpu.VMEM),
            pl.BlockSpec(memory_space=pltpu.VMEM),
        ],
        out_specs=pl.BlockSpec(memory_space=pltpu.VMEM),
        scratch_shapes=[
            pltpu.VMEM((slots, heads, capacity, width), kind),
            pltpu.VMEM((2 * rows, columns), kind),
            pltpu.VMEM((heads, 2 * rows, width), kind),
            pltpu.VMEM((2 * groups,) + bias_sides.shape[2:], jnp.float32),
            pltpu.VMEM((lists, spots, width), kind),
            pltpu.VMEM((heads * pieces, groups, piece, width), kind),
            pltpu.VMEM((heads * pieces, slots - 1, piece, width), kind),
            dma((lists,)),
            dma((heads * pieces, groups)),
            dma((heads * pieces, groups)),
            dma((heads * pieces, slots - 1)),
            dma((heads * pieces, slots - 1)),
            dma((3,)),
            dma((3,)),
            dma((3,)),
        ]
        + [pltpu.VMEM((2 * groups, piece, width), kind)] * (heads * pieces),
        cost_estimate=pl.CostEstimate(flops=int(3e10), bytes_accessed=int(1.5e8), transcendentals=0),
        compiler_params=pltpu.CompilerParams(
            collective_id=0, has_side_effects=True, vmem_limit_bytes=60 * 1024 * 1024
        ),
    )(order, places, flat_cache, queries, new_sides, bias_sides)


def attend_tile(first_query, second_query, received, bias, new_rows):
    blocks, capacity, width = received.shape
    rows, hd = first_query.shape
    q = jnp.concatenate([first_query, second_query], axis=0)
    keys = received[:, :, :hd].reshape(blocks * capacity, hd)
    values = received[:, :, hd:].reshape(blocks * capacity, hd)
    new_keys = new_rows[:, :hd]
    new_values = new_rows[:, hd:]
    scale = hd**-0.5 * math.log2(math.e)
    dims = (((1,), (1,)), ((), ()))
    kept_scores = lax.dot_general(q, keys, dims, preferred_element_type=jnp.float32) * scale
    kept_scores = kept_scores + bias
    new_scores = lax.dot_general(q, new_keys, dims, preferred_element_type=jnp.float32) * scale
    row_ids = lax.rem(lax.broadcasted_iota(jnp.int32, new_scores.shape, 0), rows)
    key_ids = lax.broadcasted_iota(jnp.int32, new_scores.shape, 1)
    new_scores = jnp.where(key_ids <= row_ids, new_scores, neg_large)
    top = jnp.maximum(
        jnp.max(kept_scores, axis=1, keepdims=True), jnp.max(new_scores, axis=1, keepdims=True)
    )
    kept_weights = jnp.exp2(kept_scores - top)
    new_weights = jnp.exp2(new_scores - top)
    total = jnp.sum(kept_weights, axis=1, keepdims=True) + jnp.sum(new_weights, axis=1, keepdims=True)
    weighted = jnp.dot(
        kept_weights.astype(jnp.bfloat16), values, preferred_element_type=jnp.float32
    ) + jnp.dot(new_weights.astype(jnp.bfloat16), new_values, preferred_element_type=jnp.float32)
    result = (weighted / total).astype(first_query.dtype)
    return result[:rows], result[rows:]


def gather_project_kernel(
    assign_ref, heads_ref, weight_hbm, out_ref,
    gat, weight, part, send_buf, recv_buf,
    send, recv, y_send, core_send, core_recv, weight_sem,
):
    c = lax.axis_index("ctx")
    t = lax.axis_index("tensor")
    d = lax.axis_index("dp")
    z, x = c // 2, c % 2
    zs = gat.shape[1] // 2
    rows = gat.shape[2]
    tile = part.shape[3]
    partner_x = z * 2 + 1 - x
    kept = out_ref.shape[0]

    load_weight = pltpu.make_async_copy(weight_hbm, weight, weight_sem)
    load_weight.start()
    barrier = pltpu.get_barrier_semaphore()
    for target in ({"ctx": partner_x}, {"dp": 1 - d}, {"tensor": 1 - t}):
        pl.semaphore_signal(barrier, inc=1, device_id=target, device_id_type=MESH)

    @pl.when(z > 0)
    def _():
        pl.semaphore_signal(barrier, inc=1, device_id={"ctx": c - 2}, device_id_type=MESH)

    @pl.when(z < zs - 1)
    def _():
        pl.semaphore_signal(barrier, inc=1, device_id={"ctx": c + 2}, device_id_type=MESH)

    pl.semaphore_wait(barrier, 3 + (z > 0).astype(jnp.int32) + (z < zs - 1).astype(jnp.int32))

    cut = rows // 4
    spans = ((d, 0, cut), (d, cut, rows), (1 - d, 0, rows // 2), (1 - d, rows // 2, rows))
    x_first = (0,)
    z_first = (1, 2, 3)

    def copy(piece, slot, channel):
        col, low, high = spans[piece]
        ref = gat.at[col, slot, pl.ds(low, high - low)]
        target = (c + 2, c - 2, partner_x)[channel]
        return pltpu.make_async_remote_copy(
            src_ref=ref, dst_ref=ref, send_sem=send.at[piece, slot, channel],
            recv_sem=recv.at[piece, slot], device_id={"ctx": target}, device_id_type=MESH,
        )

    def up(piece, slot):
        @pl.when(z < zs - 1)
        def _():
            copy(piece, slot, 0).start()

    def down(piece, slot):
        @pl.when(z > 0)
        def _():
            copy(piece, slot, 1).start()

    def arrived(piece, slot):
        copy(piece, slot, 2).wait_recv()

    def y_copy(piece):
        _, low, high = spans[piece]
        return pltpu.make_async_remote_copy(
            src_ref=heads_ref.at[pl.ds(pl.multiple_of((1 - d) * rows + low, 16), high - low)],
            dst_ref=gat.at[d, c, pl.ds(low, high - low)],
            send_sem=y_send.at[piece - 2], recv_sem=recv.at[piece, c],
            device_id={"dp": 1 - d}, device_id_type=MESH,
        )

    y_copy(2).start()
    y_copy(3).start()
    gat[d, c] = heads_ref[pl.ds(pl.multiple_of(d * rows, rows), rows)]
    copy(0, c, 2).start()
    up(1, c)
    down(1, c)
    copy(1, c, 2).start()
    up(0, c)
    down(0, c)
    for piece in (2, 3):
        arrived(piece, c)
        up(piece, c)
        down(piece, c)
        copy(piece, c, 2).start()
    arrived(0, partner_x)
    up(0, partner_x)
    down(0, partner_x)
    slots = gat.shape[1]
    depth = gat.shape[3]
    tiles = part.shape[0]
    near = z // 2 * (slots // 2)
    far = slots // 2 - near

    def multiply(n, first):
        span = pl.ds(pl.multiple_of(n * tile, tile), tile)
        some = pl.ds(first, slots // 2)
        flat = (slots // 2 * rows, depth)
        product = jnp.dot(
            gat[0, some].reshape(flat), weight[:depth, span], preferred_element_type=jnp.float32
        ) + jnp.dot(
            gat[1, some].reshape(flat), weight[depth:, span], preferred_element_type=jnp.float32
        )
        part[n, some] = product.reshape(slots // 2, rows, tile)

    for k in range(1, zs):
        if k == zs - 1:
            for piece in z_first:
                for zo in range(2):
                    arrived(piece, near + zo * 2 + 1 - x)
            load_weight.wait()
        for index, piece in enumerate((1, 0, 2, 3)):
            if k == zs - 1:
                for n in range(index * tiles // 4, (index + 1) * tiles // 4):
                    multiply(n, near)
            for base in (c, partner_x) if piece in x_first else (c,):
                @pl.when(z >= k)
                def _():
                    arrived(piece, base - 2 * k)
                    up(piece, base - 2 * k)
                    if piece in z_first:
                        copy(piece, base - 2 * k, 2).start()

                @pl.when(z + k < zs)
                def _():
                    arrived(piece, base + 2 * k)
                    down(piece, base + 2 * k)
                    if piece in z_first:
                        copy(piece, base + 2 * k, 2).start()

    for piece in z_first:
        for zo in range(2):
            arrived(piece, far + zo * 2 + 1 - x)

    def exchange(n):
        return pltpu.make_async_remote_copy(
            src_ref=send_buf.at[n], dst_ref=recv_buf.at[n], send_sem=core_send.at[n],
            recv_sem=core_recv.at[n], device_id={"tensor": 1 - t}, device_id_type=MESH,
        )

    def tile_step(n, carry):
        multiply(n, far)
        for j in range(kept):
            send_buf[n, j] = part[n, assign_ref[(1 - t) * kept + j]].astype(send_buf.dtype)
        exchange(n).start()
        return carry

    lax.fori_loop(0, tiles, tile_step, 0)
    for n in range(tiles):
        exchange(n).wait_recv()
        for j in range(kept):
            total = part[n, assign_ref[t * kept + j]] + recv_buf[n, j].astype(jnp.float32)
            out_ref[j, :, n * tile : (n + 1) * tile] = total.astype(out_ref.dtype)

    y_copy(2).wait_send()
    y_copy(3).wait_send()
    for n in range(tiles):
        exchange(n).wait_send()
    for piece in x_first + z_first:
        copy(piece, c, 2).wait_send()
        for base in (c, partner_x) if piece in x_first else (c,):
            @pl.when(z < zs - 1)
            def _():
                copy(piece, base, 0).wait_send()

            @pl.when(z > 0)
            def _():
                copy(piece, base, 1).wait_send()

            for k in range(1, zs):
                @pl.when(z >= k)
                def _():
                    if piece in z_first:
                        copy(piece, base - 2 * k, 2).wait_send()

                    @pl.when(z < zs - 1)
                    def _():
                        copy(piece, base - 2 * k, 0).wait_send()

                @pl.when(z + k < zs)
                def _():
                    if piece in z_first:
                        copy(piece, base + 2 * k, 2).wait_send()

                    @pl.when(z > 0)
                    def _():
                        copy(piece, base + 2 * k, 1).wait_send()


def gather_project(head_out, out_weight, assign):
    slots = assign.shape[0]
    rows, half_depth = head_out.shape[0] // 2, head_out.shape[1]
    depth, columns = out_weight.shape
    kept = slots // 2
    tile = 256
    tiles = columns // tile
    kind = head_out.dtype
    dma = pltpu.SemaphoreType.DMA
    return pl.pallas_call(
        gather_project_kernel,
        out_shape=jax.ShapeDtypeStruct((kept, rows, columns), kind),
        in_specs=[
            pl.BlockSpec(memory_space=pltpu.SMEM),
            pl.BlockSpec(memory_space=pltpu.VMEM),
            pl.BlockSpec(memory_space=pl.ANY),
        ],
        out_specs=pl.BlockSpec(memory_space=pltpu.VMEM),
        scratch_shapes=[
            pltpu.VMEM((2, slots, rows, half_depth), kind),
            pltpu.VMEM((depth, columns), kind),
            pltpu.VMEM((tiles, slots, rows, tile), jnp.float32),
            pltpu.VMEM((tiles, kept, rows, tile), kind),
            pltpu.VMEM((tiles, kept, rows, tile), kind),
            dma((4, slots, 3)),
            dma((4, slots)),
            dma((2,)),
            dma((tiles,)),
            dma((tiles,)),
            dma,
        ],
        compiler_params=pltpu.CompilerParams(
            collective_id=1, has_side_effects=True, vmem_limit_bytes=48 * 1024 * 1024
        ),
    )(assign, head_out, out_weight)


def local(cache, kept, assign, queries, new_kv, out_weight):
    groups, kv_here, ctx_dev, width = cache.shape
    ctx_count = lax.axis_size("ctx")
    if kv_here % 2 or ctx_count != 8 or lax.axis_size("tensor") != 2:
        return local_by_rows(cache, kept, assign, queries, new_kv, out_weight)
    ctx_id = lax.axis_index("ctx")
    capacity = ctx_dev // 2
    heads = kv_here // 2
    rows = queries.shape[1]
    slots = jnp.arange(assign.shape[0], dtype=jnp.int32)
    order = jnp.sum(jnp.where(assign[None, :] == slots[:, None], slots[None, :], 0), axis=1)
    edges = ctx_dev * jnp.arange(ctx_count + 1, dtype=jnp.int32)
    below = jnp.sum((kept[:, :, None, :] < edges[:, None]).astype(jnp.int32), axis=3)
    counts = below[:, :, 1:] - below[:, :, :-1]
    counts = jnp.transpose(counts.reshape(groups, 2, heads, ctx_count), (1, 0, 2, 3))
    offsets = jnp.arange(capacity, dtype=jnp.int32)
    bias = jnp.where(offsets < counts[..., None], 0.0, neg_large).astype(jnp.float32)
    bias = bias.reshape(2, groups, heads, ctx_count * capacity)
    new_sides = jnp.transpose(new_kv[0], (1, 0, 2)).reshape(2, heads, rows, width)
    places = places_of(kept, ctx_id * ctx_dev, capacity)
    flat_cache = cache.reshape(groups * kv_here, ctx_dev, width)
    head_out = relayout_attend(flat_cache, places, order, groups, queries[0], new_sides, bias)
    return gather_project(head_out, out_weight, assign)


def solution(mesh):
    placed = (
        P("dp", "tensor", "ctx", None),
        P("dp", "tensor", None),
        P(),
        P("ctx", "dp", "tensor"),
        P("ctx", "dp", "tensor", None),
        P("tensor", "ctx"),
    )
    return jax.shard_map(
        local, mesh=mesh, in_specs=placed, out_specs=P("tensor", "dp", "ctx"), check_vma=False
    )
```
